32 devices in a mesh: head: 4 (over z), pool: 8 (over y, x, core).
Axes of the slice: x: 2, y: 2, z: 4, core: 2. Of those that a mesh axis runs over, the one named last changes fastest.
Arguments:
- queries: bfloat16 [80, 2048], P('pool', 'head'), may hold values from -6 to 6
- fresh_pair: bfloat16 [80, 2, 2048], P('pool', None, 'head'), may hold values from -6 to 6
- cache_blocks: bfloat16 [288, 2, 64, 2048], P('pool', None, None, 'head'), may hold values from -6 to 6
- block_table: int32 [80, 64], replicated, may hold values from -1 to 287, as said below
- lengths: int32 [80], replicated, may hold values from 65 to 4096, as said below
- residual: bfloat16 [80, 2048], P('pool'), may hold values from -6 to 6
- w_output: bfloat16 [2048, 2048], P('head'), may hold values from -0.125 to 0.125
- norm_gain: bfloat16 [2048], replicated, may hold values from 0.5 to 1.5
- routes: int32 [80, 6], replicated, may hold values from 0 to 63, all different within a row; in each aligned block of 10 rows (0 to 9, 10 to 19, ...) at most 2 rows name the same one
- route_gates: float32 [80, 6], replicated, may hold values from 0.1 to 0.6
- w_gate_up: bfloat16 [64, 2048, 2, 1408], P('pool', 'head'), may hold values from -0.125 to 0.125
- w_down: bfloat16 [64, 1408, 2048], P('pool', None, 'head'), may hold values from -0.15625 to 0.15625
- shared_gate_up: bfloat16 [1, 2048, 2, 1408], P(None, 'head'), may hold values from -0.125 to 0.125
- shared_down: bfloat16 [1, 1408, 2048], P(None, None, 'head'), may hold values from -0.15625 to 0.15625
- next_gain: bfloat16 [2048], replicated, may hold values from 0.5 to 1.5
- w_query_key_value: bfloat16 [2048, 6144], P(None, 'head'), may hold values from -0.125 to 0.125
Outputs:
- next_hidden: bfloat16 [80, 2048], P('pool')
- next_query_key_value: bfloat16 [80, 6144], P('pool', 'head')
The draws below stay inside these ranges and needn't reach their ends.
Inputs may be any that keep to these rules, and one draw needn't show every extreme that they name: `block_table`: row r lists request r's blocks in order, then -1; 2 requests have 64 blocks and the others 2; no block is listed twice; block g lies on pool device g // 36. `lengths`: A request with n blocks holds (n - 1) * 64 + 1 to n * 64 tokens; some request holds 4096. `routes`: each row names 6 different experts; within the 10 rows of one pool device no expert is named more than 2 times, a bound that some block reaches.
All inputs are finite; a program needn't handle non-finite values.
Results may differ from the reference program's by a relative error of at most 0.025.
Values may be sent and summed in bfloat16 or wider, within the bound.
No kernel may reach another device: no remote copies, remote signals or barrier semaphores. Data moves between devices by JAX's collectives and lax.ppermute only.
A program may use at most 128 MiB of HBM per device.

```python
import math
import jax
import jax.numpy as jnp
import numpy as np
from jax import lax

D = 2048
H = 16
HD = 128
EXP = 64
FFE = 1408
TOPK = 6
NSH = 1
BS = 64
SB = 2
R_LONG = 2
REQ_DEV = 10
MOST = 2
REQ = 80
LONG_BLOCKS = 64
BLK_DEV = 36
NBLK = 288
N_POOL = 8


def table_and_lengths(key):
    base = jax.random.fold_in(key, 301)
    order = jax.random.permutation(jax.random.fold_in(base, 1), REQ).astype(jnp.int32)
    is_long = jnp.zeros((REQ,), jnp.int32).at[order[:R_LONG]].set(1)
    counts = jnp.where(is_long == 1, LONG_BLOCKS, SB).astype(jnp.int32)
    offsets = jnp.cumsum(counts) - counts
    shuffled = jax.random.permutation(jax.random.fold_in(base, 2), NBLK).astype(jnp.int32)
    columns = jnp.arange(LONG_BLOCKS, dtype=jnp.int32)
    picks = jnp.minimum(offsets[:, None] + columns[None, :], NBLK - 1).astype(jnp.int32)
    table = jnp.where(columns[None, :] < counts[:, None], shuffled[picks], -1).astype(jnp.int32)
    tail = jax.random.randint(jax.random.fold_in(base, 3), (REQ,), 1, BS + 1).astype(jnp.int32)
    token_counts = (counts - 1) * BS + tail
    full_one = order[0]
    token_counts = jnp.where(jnp.arange(REQ, dtype=jnp.int32) == full_one, counts * BS, token_counts)
    return (table, token_counts.astype(jnp.int32))


def draw_block_table(key, part):
    return table_and_lengths(key)[0]


def draw_lengths(key, part):
    return table_and_lengths(key)[1]


def draw_queries(key, part):
    noise = jax.random.normal(jax.random.fold_in(key, 11), (REQ, H * HD), jnp.float32)
    values = noise
    return jnp.clip(values, -6.0, 6.0).astype(jnp.bfloat16)


def draw_cache_blocks(key, part):
    values = jax.random.normal(jax.random.fold_in(key, 21), (NBLK, 2, BS, H * HD), jnp.float32)
    return jnp.clip(values, -6.0, 6.0).astype(jnp.bfloat16)


def block_scale(rng, extent, pieces, least, top_value):
    def one(axis_at, blocks):
        draws = jax.random.uniform(jax.random.fold_in(jax.random.fold_in(rng, 6), axis_at), (blocks,), jnp.float32, least / len(pieces), top_value / len(pieces))
        return jnp.repeat(jnp.exp(draws), extent[axis_at] // blocks).reshape((-1,) + (1,) * (len(extent) - axis_at - 1))

    factor_of = one(*pieces[0])
    for cut in pieces[1:]:
        factor_of = factor_of * one(*cut)
    return factor_of


def routed_block(stream_key, own, number, rows, count, top, limit, lean):
    sequence = jax.random.permutation(stream_key, count)
    packed, common = load_shares(count, rows * top, limit, lean, True), load_shares(count, rows * top, limit, lean, False)
    places = jnp.arange(count)

    def named(sizes, turn):
        used = int((sizes > 0).sum())
        fixed = max(1, used // 4)
        shifted = fixed + (places - fixed + turn * (used - fixed)) % max(1, count - fixed)
        return jnp.zeros((count,), jnp.int32).at[sequence[jnp.where(places < fixed, places, shifted)]].set(jnp.asarray(sizes, jnp.int32))

    sizes = jnp.where(number % 4 == 0, named(packed, number // 4), named(common, number - number // 4 - 1))
    mixed = jax.random.permutation(jax.random.fold_in(own, 3), count)
    donor, receiver = mixed[0:count // 2 * 2:2], mixed[1:count // 2 * 2:2]
    margin = jnp.minimum(sizes[donor] - 1, limit - sizes[receiver]) // 2
    margin = jnp.where((donor == sequence[0]) | (receiver == sequence[0]) | (sizes[receiver] == 0), 0, jnp.maximum(margin, 0))
    shifted = jax.random.randint(jax.random.fold_in(own, 4), (count // 2,), 0, 1 << 20) % (margin + 1)
    sizes = sizes.at[donor].add(-shifted).at[receiver].add(shifted)
    items = jnp.searchsorted(jnp.cumsum(sizes), jnp.arange(rows * top), side="right").astype(jnp.int32)
    listing = items.reshape(top, rows).T
    listing = listing[jax.random.permutation(jax.random.fold_in(own, 1), rows)]
    turn = jax.random.randint(jax.random.fold_in(own, 2), (rows, 1), 0, top)
    return jnp.take_along_axis(listing, (jnp.arange(top)[None, :] + turn) % top, axis=1)


def load_shares(number_of, total, limit, lean, full):
    weights = [(1 << 20) // math.isqrt(standing ** lean) + 1 for standing in range(1, number_of + 1)]
    largest = limit if full else min(limit, max(-(-total // number_of), total * weights[0] // sum(weights)))
    least = 1 if total - largest >= number_of - 1 else 0
    given, spare = [largest] + [least] * (number_of - 1), total - largest - least * (number_of - 1)
    while spare > 0:
        candidates = [i for i in range(1, number_of) if given[i] < largest] or [i for i in range(1, number_of) if given[i] < limit]
        pool, budget = sum([weights[i] for i in candidates]), spare
        for i in candidates:
            more = min(limit - given[i], max(1, budget * weights[i] // pool), spare)
            given[i] = given[i] + more
            spare = spare - more
    return np.array(given)


def scatter_about(stream_key, shape, scale, limit, shards=(), kind=jnp.bfloat16):
    result = jax.random.normal(stream_key, shape, jnp.float32) * scale
    if len(shards) > 0:
        result = block_scale(stream_key, shape, shards, -0.22, 0.18) * result
    return jnp.clip(result, min=-limit, max=limit).astype(kind)


def setup_inputs(seed: int = 0) -> dict:
    key_list = jax.random.split(jax.random.key(seed), 17)
    queries = draw_queries(jax.random.fold_in(key_list[16], 71), 0)
    fresh_pair = scatter_about(key_list[1], (REQ, 2, H * HD), 1.0, 6.0, ((0, 8), (2, 4)))
    cache_blocks = draw_cache_blocks(jax.random.fold_in(key_list[16], 71), 0)
    block_table = draw_block_table(jax.random.fold_in(key_list[16], 71), 0)
    lengths = draw_lengths(jax.random.fold_in(key_list[16], 71), 0)
    residual = scatter_about(key_list[5], (REQ, D), 1.0, 6.0, ((0, 8),))
    w_output = scatter_about(key_list[6], (H * HD, D), (H * HD) ** -0.5, 0.125, ((0, 4),))
    norm_gain = jnp.clip(1.0 + 0.1 * jax.random.normal(key_list[7], (D,), jnp.float32), 0.5, 1.5).astype(jnp.bfloat16)
    routes_keys = jax.random.split(jax.random.fold_in(key_list[8], 1), REQ // REQ_DEV)
    routes_turns = jax.random.permutation(jax.random.fold_in(key_list[8], 3), REQ // REQ_DEV)
    routes = jax.vmap(lambda own, number: routed_block(jax.random.fold_in(key_list[8], 2), own, number, REQ_DEV, EXP, TOPK, MOST, 2))(routes_keys, routes_turns).reshape((REQ, TOPK))
    route_gates = jnp.clip(jax.random.uniform(key_list[9], (REQ, TOPK), jnp.float32, 0.1, 0.6), 0.1, 0.6)
    w_gate_up = scatter_about(key_list[10], (EXP, D, 2, FFE), D ** -0.5, 0.125, ((0, 8), (1, 4)))
    w_down = scatter_about(key_list[11], (EXP, FFE, D), FFE ** -0.5, 0.15625, ((0, 8), (2, 4)))
    shared_gate_up = scatter_about(key_list[12], (NSH, D, 2, FFE), D ** -0.5, 0.125, ((1, 4),))
    shared_down = scatter_about(key_list[13], (NSH, FFE, D), FFE ** -0.5, 0.15625, ((2, 4),))
    next_gain = jnp.clip(1.0 + 0.1 * jax.random.normal(key_list[14], (D,), jnp.float32), 0.5, 1.5).astype(jnp.bfloat16)
    w_query_key_value = scatter_about(key_list[15], (D, 3 * H * HD), D ** -0.5, 0.125, ((1, 4),))
    return {"queries": queries, "fresh_pair": fresh_pair, "cache_blocks": cache_blocks, "block_table": block_table, "lengths": lengths, "residual": residual, "w_output": w_output, "norm_gain": norm_gain, "routes": routes, "route_gates": route_gates, "w_gate_up": w_gate_up, "w_down": w_down, "shared_gate_up": shared_gate_up, "shared_down": shared_down, "next_gain": next_gain, "w_query_key_value": w_query_key_value}


epsilon = 1e-06
floor_score = -1e+30

def norm_rows(values, gain):
    mean_square = lax.optimization_barrier(jnp.mean(values * values, axis=-1, keepdims=True))
    return values * lax.rsqrt(mean_square + epsilon) * gain.astype(jnp.float32)

def block_owners(block_table):
    req_total, list_len = block_table.shape
    row_ids = jnp.broadcast_to(jnp.arange(req_total, dtype=jnp.int32)[:, None], (req_total, list_len)).reshape(-1)
    col_ids = jnp.broadcast_to(jnp.arange(list_len, dtype=jnp.int32)[None, :], (req_total, list_len)).reshape(-1)
    target = jnp.where(block_table >= 0, block_table, NBLK).reshape(-1).astype(jnp.int32)
    owners = jnp.full((NBLK + 1,), req_total, jnp.int32).at[target].set(row_ids)[:NBLK]
    ranks = jnp.zeros((NBLK + 1,), jnp.int32).at[target].set(col_ids)[:NBLK]
    return (owners, ranks)

def attention(queries, fresh_pair, cache_blocks, block_table, lengths):
    owners, ranks = block_owners(block_table)
    score_scale = 1.0 / math.sqrt(HD)
    query_rows = queries.astype(jnp.float32).reshape(REQ, H, HD)
    fresh_keys = fresh_pair[:, 0].astype(jnp.float32).reshape(REQ, H, HD)
    fresh_values = fresh_pair[:, 1].astype(jnp.float32).reshape(REQ, H, HD)
    fresh_score = lax.optimization_barrier(jnp.sum(query_rows * fresh_keys, axis=-1)) * score_scale
    safe_owner = jnp.minimum(owners, REQ - 1).astype(jnp.int32)
    token_pos = ranks[:, None] * BS + jnp.arange(BS, dtype=jnp.int32)[None, :]
    usable = jnp.logical_and(owners[:, None] < REQ, token_pos < lengths[safe_owner][:, None])
    grouped = cache_blocks.reshape(N_POOL, BLK_DEV, 2, BS, H, HD)
    owner_groups = safe_owner.reshape(N_POOL, BLK_DEV)
    usable_groups = usable.reshape(N_POOL, BLK_DEV, BS)

    def group_scores(blocks, owner_ids, alive):
        picked = query_rows[owner_ids]
        raw = jnp.einsum('bjhd,bhd->bjh', blocks[:, 0].astype(jnp.float32), picked) * score_scale
        return jnp.where(alive[:, :, None], raw, floor_score)

    def group_max(args):
        return lax.optimization_barrier(jnp.max(group_scores(args[0], args[1], args[2]), axis=1))
    block_max = lax.map(group_max, (grouped, owner_groups, usable_groups)).reshape(NBLK, H)
    is_owner = owners[None, :] == jnp.arange(REQ, dtype=jnp.int32)[:, None]
    top = lax.optimization_barrier(jnp.max(jnp.where(is_owner[:, :, None], block_max[None], floor_score), axis=1))
    top = jnp.maximum(top, fresh_score)
    top_groups = top[owner_groups]

    def group_sums(args):
        blocks, owner_ids, alive, shift = args
        weights_exp = jnp.where(alive[:, :, None], jnp.exp(group_scores(blocks, owner_ids, alive) - shift[:, None, :]), 0.0)
        block_total = lax.optimization_barrier(jnp.sum(weights_exp, axis=1))
        block_acc = jnp.einsum('bjh,bjhd->bhd', weights_exp, blocks[:, 1].astype(jnp.float32))
        return (block_total, block_acc)
    block_total, block_acc = lax.map(group_sums, (grouped, owner_groups, usable_groups, top_groups))
    segment = jnp.where(owners < REQ, owners, REQ).astype(jnp.int32)
    fresh_weight = jnp.exp(fresh_score - top)
    denom = jax.ops.segment_sum(block_total.reshape(NBLK, H), segment, num_segments=REQ + 1)[:REQ] + fresh_weight
    numer = jax.ops.segment_sum(block_acc.reshape(NBLK, H, HD), segment, num_segments=REQ + 1)[:REQ]
    numer = numer + fresh_weight[:, :, None] * fresh_values
    return (numer / denom[:, :, None]).astype(jnp.bfloat16).reshape(REQ, H * HD)

def routed_terms(normed, routes, route_gates, w_gate_up, w_down):

    def one_token(args):
        row, chosen, weights = args
        preact = jnp.einsum('d,kdcf->kcf', row.astype(jnp.float32), w_gate_up[chosen].astype(jnp.float32))
        hidden = (jax.nn.silu(preact[:, 0]) * preact[:, 1]).astype(jnp.bfloat16)
        expert_out = jnp.einsum('kf,kfd->kd', hidden.astype(jnp.float32), w_down[chosen].astype(jnp.float32))
        return lax.optimization_barrier(jnp.sum(expert_out * weights[:, None], axis=0))
    return lax.map(one_token, (normed, routes, route_gates))

def shared_terms(normed, shared_gate_up, shared_down):
    preact = jnp.einsum('td,sdcf->tscf', normed.astype(jnp.float32), shared_gate_up.astype(jnp.float32))
    shared_hidden = (jax.nn.silu(preact[:, :, 0]) * preact[:, :, 1]).astype(jnp.bfloat16)
    return jnp.einsum('tsf,sfd->td', shared_hidden.astype(jnp.float32), shared_down.astype(jnp.float32))

def reference(queries, fresh_pair, cache_blocks, block_table, lengths, residual, w_output, norm_gain, routes, route_gates, w_gate_up, w_down, shared_gate_up, shared_down, next_gain, w_query_key_value):
    attended = attention(queries, fresh_pair, cache_blocks, block_table, lengths)
    after_attention = residual.astype(jnp.float32) + jnp.dot(attended, w_output, preferred_element_type=jnp.float32)
    normed = norm_rows(after_attention, norm_gain).astype(jnp.bfloat16)
    routed = routed_terms(normed, routes, route_gates, w_gate_up, w_down)
    shared_out = shared_terms(normed, shared_gate_up, shared_down)
    after_ffn = after_attention + routed + shared_out
    next_normed = norm_rows(after_ffn, next_gain).astype(jnp.bfloat16)
    projected = jnp.dot(next_normed, w_query_key_value, preferred_element_type=jnp.float32).astype(jnp.bfloat16)
    return (after_ffn.astype(jnp.bfloat16), projected)
```

```python
import functools
import math

import jax
import jax.numpy as jnp
from jax import lax
from jax.experimental import pallas as pl
from jax.experimental.pallas import tpu as pltpu
from jax.sharding import PartitionSpec as P

HD = 128
LANES = 128
MOST = 2


epsilon = 1e-06
floor_score = -1e30
bf16 = jnp.bfloat16
f32 = jnp.float32


def swap(value, axis, distance):
    count = lax.axis_size(axis)
    return lax.ppermute(value, axis, [(i, i ^ distance) for i in range(count)])


def gather_xor(value, axis):
    count = lax.axis_size(axis)
    held = value[None]
    distance = 1
    while distance < count:
        held = jnp.concatenate([held, swap(held, axis, distance)], axis=0)
        distance *= 2
    return held


def gather_ordered(value, axis):
    held = gather_xor(value, axis)
    me = lax.axis_index(axis)
    return jnp.stack(
        [
            lax.dynamic_index_in_dim(held, me ^ place, 0, keepdims=False)
            for place in range(held.shape[0])
        ]
    )


def scatter_sum(chunks, axis):
    count = lax.axis_size(axis)
    me = lax.axis_index(axis)
    sent = [
        swap(lax.dynamic_index_in_dim(chunks, me ^ distance, 0, keepdims=False), axis, distance)
        for distance in range(1, count)
    ]
    total = lax.dynamic_index_in_dim(chunks, me, 0, keepdims=False).astype(f32)
    for piece in sent:
        total = total + piece.astype(f32)
    return total


def attention_kernel(place_ref, query_ref, cache_ref, limit_ref, fresh_ref, out_ref):
    req_total, lane_width = query_ref.shape
    blocks, _, block_len, _ = cache_ref.shape
    fresh_rows = fresh_ref.shape[1]
    tokens = blocks * block_len
    scale = 1.0 / math.sqrt(HD)
    block_of = lax.broadcasted_iota(jnp.int32, (blocks, tokens), 1) // block_len
    expand = block_of == lax.broadcasted_iota(jnp.int32, (blocks, tokens), 0)
    limits = jnp.dot(
        limit_ref[...], expand.astype(f32).astype(bf16), preferred_element_type=f32
    )
    within = lax.rem(lax.broadcasted_iota(jnp.int32, (req_total, tokens), 1), block_len)
    live = within.astype(f32) < limits
    row_ids = lax.broadcasted_iota(jnp.int32, (req_total, fresh_rows), 0)
    column_ids = lax.broadcasted_iota(jnp.int32, (req_total, fresh_rows), 1)
    req_dev = place_ref[1]
    own = jnp.logical_and(row_ids == column_ids + place_ref[0], column_ids < req_dev)
    lane = lax.broadcasted_iota(jnp.int32, (req_total, LANES), 1)
    side = jnp.zeros((req_total, LANES), f32)
    heads = lane_width // HD
    for head in range(heads):
        columns = slice(head * HD, (head + 1) * HD)
        query = query_ref[:, columns]
        keys = cache_ref[:, 0, :, columns].reshape(tokens, HD)
        values = cache_ref[:, 1, :, columns].reshape(tokens, HD)
        contract = (((1,), (1,)), ((), ()))
        scores = lax.dot_general(query, keys, contract, preferred_element_type=f32) * scale
        scores = jnp.where(live, scores, floor_score)
        new_scores = (
            lax.dot_general(query, fresh_ref[0, :, columns], contract, preferred_element_type=f32)
            * scale
        )
        new_scores = jnp.where(own, new_scores, floor_score)
        top = jnp.maximum(
            jnp.max(scores, axis=1, keepdims=True), jnp.max(new_scores, axis=1, keepdims=True)
        )
        top = top.astype(bf16).astype(f32)
        weights = jnp.where(live, jnp.exp(scores - top), 0.0)
        new_weights = jnp.where(own, jnp.exp(new_scores - top), 0.0)
        total = jnp.sum(weights, axis=1, keepdims=True) + jnp.sum(
            new_weights, axis=1, keepdims=True
        )
        mixed = jnp.dot(weights.astype(bf16), values, preferred_element_type=f32) + jnp.dot(
            new_weights.astype(bf16), fresh_ref[1, :, columns], preferred_element_type=f32
        )
        inverse = jnp.where(total > 0.0, 1.0 / jnp.where(total > 0.0, total, 1.0), 0.0)
        out_ref[:, columns] = (mixed * inverse).astype(bf16)
        coarse = total.astype(bf16).astype(f32)
        side = jnp.where(lane == head, top, side)
        side = jnp.where(lane == heads + head, coarse, side)
        side = jnp.where(lane == 2 * heads + head, total - coarse, side)
    out_ref[:, lane_width:] = side.astype(bf16)


def merge_kernel(parts_ref, weight_ref, out_ref, attended_ref):
    count, req_total, packed = parts_ref.shape
    lane_width = packed - LANES
    heads = lane_width // HD
    chunks, _, chunk_width = out_ref.shape
    lane = lax.broadcasted_iota(jnp.int32, (req_total, LANES), 1)
    sides = [parts_ref[i, :, lane_width:].astype(f32) for i in range(count)]

    def column(side, place):
        return jnp.sum(jnp.where(lane == place, side, 0.0), axis=1, keepdims=True)

    for head in range(heads):
        columns = slice(head * HD, (head + 1) * HD)
        tops = [column(side, head) for side in sides]
        totals = [column(side, heads + head) + column(side, 2 * heads + head) for side in sides]
        top = functools.reduce(jnp.maximum, tops)
        shares = [total * jnp.exp(part - top) for part, total in zip(tops, totals)]
        denominator = functools.reduce(jnp.add, shares)
        mixed = functools.reduce(
            jnp.add,
            [shares[i] * parts_ref[i, :, columns].astype(f32) for i in range(count)],
        )
        attended_ref[:, columns] = (mixed / denominator).astype(bf16)
    for chunk in range(chunks):
        out_ref[chunk] = jnp.dot(
            attended_ref[...],
            weight_ref[:, chunk * chunk_width : (chunk + 1) * chunk_width],
            preferred_element_type=f32,
        ).astype(bf16)


def norm_rows(values, gain):
    mean_square = jnp.mean(values * values, axis=-1, keepdims=True)
    return values * lax.rsqrt(mean_square + epsilon) * gain.astype(f32)


def split_float(value):
    coarse = value.astype(bf16)
    return coarse, (value - coarse.astype(f32)).astype(bf16)


def per_device(
    queries,
    fresh_pair,
    cache_blocks,
    block_table,
    lengths,
    residual,
    w_output,
    norm_gain,
    routes,
    route_gates,
    w_gate_up,
    w_down,
    shared_gate_up,
    shared_down,
    next_gain,
    w_query_key_value,
):
    pool_idx = lax.axis_index("pool")
    head_idx = lax.axis_index("head")
    pools = lax.axis_size("pool")
    head_devs = lax.axis_size("head")
    req_dev, lane_width = queries.shape
    req_total, list_len = block_table.shape
    blk_count, _, block_len, _ = cache_blocks.shape
    exp_dev, col_part, _, ffe = w_gate_up.shape
    width = residual.shape[1]
    row_start = pool_idx * req_dev
    col_start = head_idx * col_part

    residual_part = lax.dynamic_slice_in_dim(residual, col_start, col_part, 1)
    gathered = lax.all_gather(
        jnp.concatenate([queries, residual_part], axis=1), "pool", axis=0, tiled=True
    )
    all_queries = gathered[:, :lane_width]
    all_residual = gathered[:, lane_width:].astype(f32)

    block_ids = pool_idx * blk_count + jnp.arange(blk_count, dtype=jnp.int32)
    left = lengths[:, None] - jnp.arange(list_len, dtype=jnp.int32)[None, :] * block_len
    limits = jnp.sum(
        jnp.where(block_table[:, None, :] == block_ids[None, :, None], left[:, None, :], 0), axis=2
    )
    limits = jnp.clip(limits, 0, block_len).astype(bf16)
    fresh_rows = -(-req_dev // 16) * 16
    fresh = jnp.pad(jnp.swapaxes(fresh_pair, 0, 1), ((0, 0), (0, fresh_rows - req_dev), (0, 0)))
    place = jnp.stack([row_start, jnp.int32(req_dev)]).astype(jnp.int32)
    vmem = pl.BlockSpec(memory_space=pltpu.VMEM)
    partial = pl.pallas_call(
        attention_kernel,
        out_shape=jax.ShapeDtypeStruct((req_total, lane_width + LANES), bf16),
        in_specs=[pl.BlockSpec(memory_space=pltpu.SMEM)] + [vmem] * 4,
        out_specs=vmem,
        compiler_params=pltpu.CompilerParams(vmem_limit_bytes=40 * 1024 * 1024),
        name="attention",
    )(place, all_queries, cache_blocks, limits, fresh)

    parts = lax.all_gather(partial, "pool", axis=0)
    projected = pl.pallas_call(
        merge_kernel,
        out_shape=jax.ShapeDtypeStruct((head_devs, req_total, col_part), bf16),
        in_specs=[vmem] * 2,
        out_specs=vmem,
        scratch_shapes=[pltpu.VMEM((req_total, lane_width), bf16)],
        compiler_params=pltpu.CompilerParams(vmem_limit_bytes=40 * 1024 * 1024),
        name="merge_project",
    )(parts, w_output)
    after_attention = all_residual + scatter_sum(projected, "head")

    gain_part = lax.dynamic_slice_in_dim(norm_gain, col_start, col_part, 0).astype(f32)
    scaled = (after_attention * gain_part[None, :]).astype(bf16)
    squares = jnp.sum(after_attention * after_attention, axis=1, keepdims=True)
    coarse, fine = split_float(squares)
    side = jnp.pad(jnp.concatenate([coarse, fine], axis=1), ((0, 0), (0, LANES - 2)))
    rows = jnp.concatenate([scaled, side], axis=1)

    slots = min(MOST * pools, req_total)
    local_ids = pool_idx * exp_dev + jnp.arange(exp_dev, dtype=jnp.int32)
    named = routes[:, :, None] == local_ids[None, None, :]
    gate = jnp.sum(jnp.where(named, route_gates[:, :, None], 0.0), axis=1)
    chosen = jnp.any(named, axis=1)
    earlier = jnp.tril(jnp.ones((req_total, req_total), bf16), -1)
    rank = jnp.dot(earlier, chosen.astype(bf16), preferred_element_type=f32)
    slot_ids = jnp.arange(slots, dtype=jnp.int32).astype(f32)
    pick = jnp.logical_and(
        chosen.T[:, None, :], rank.T[:, None, :] == slot_ids[None, :, None]
    )
    slot_gate = jnp.sum(jnp.where(pick, gate.T[:, None, :], 0.0), axis=2)
    pick = pick.astype(bf16)

    picked = jnp.einsum("ekt,td->ekd", pick, rows, preferred_element_type=f32).astype(bf16)
    own_rows = lax.dynamic_slice_in_dim(rows, row_start, req_dev, 0)
    routed_pre = jnp.einsum(
        "ekd,edcf->ekcf", picked[:, :, :col_part], w_gate_up, preferred_element_type=f32
    ).astype(bf16)
    shared_pre = jnp.einsum(
        "td,dcf->tcf", own_rows[:, :col_part], shared_gate_up[0], preferred_element_type=f32
    ).astype(bf16)
    shared_rows = -(-req_dev // head_devs) * head_devs
    routed_payload = jnp.concatenate(
        [routed_pre.reshape(exp_dev * slots, 2 * ffe), picked[:, :, col_part:].reshape(-1, LANES)],
        axis=1,
    ).reshape(head_devs, -1, 2 * ffe + LANES)
    shared_payload = jnp.pad(
        jnp.concatenate([shared_pre.reshape(req_dev, 2 * ffe), own_rows[:, col_part:]], axis=1),
        ((0, shared_rows - req_dev), (0, 0)),
    ).reshape(head_devs, -1, 2 * ffe + LANES)
    payload = jnp.concatenate([routed_payload, shared_payload], axis=1)
    sums = scatter_sum(payload, "head")
    square_sum = sums[:, 2 * ffe : 2 * ffe + 1] + sums[:, 2 * ffe + 1 : 2 * ffe + 2]
    row_scale = lax.rsqrt(square_sum / width + epsilon)
    gates = sums[:, :ffe] * row_scale
    ups = sums[:, ffe : 2 * ffe] * row_scale
    hidden = (jax.nn.silu(gates) * ups).astype(bf16)

    all_hidden = gather_ordered(hidden, "head")
    routed_part = routed_payload.shape[1]
    routed_hidden = all_hidden[:, :routed_part].reshape(exp_dev, slots, ffe)
    shared_hidden = all_hidden[:, routed_part:].reshape(shared_rows, ffe)
    expert_out = jnp.einsum("ekf,efd->ekd", routed_hidden, w_down, preferred_element_type=f32)
    shared_out = jnp.dot(shared_hidden, shared_down[0], preferred_element_type=f32)[:req_dev]
    weighted = (expert_out * slot_gate[:, :, None]).astype(bf16)
    routed = jnp.einsum("ekt,ekd->td", pick, weighted, preferred_element_type=f32)
    pieces = lax.all_to_all(
        routed.astype(bf16).reshape(pools, req_dev, col_part), "pool", 0, 0
    )
    own_after = lax.dynamic_slice_in_dim(after_attention, row_start, req_dev, 0)
    block = own_after + shared_out + jnp.sum(pieces.astype(f32), axis=0)

    after_ffn = gather_ordered(block, "head")
    after_ffn = jnp.swapaxes(after_ffn, 0, 1).reshape(req_dev, width)
    next_normed = norm_rows(after_ffn, next_gain).astype(bf16)
    next_projection = jnp.dot(
        next_normed, w_query_key_value, preferred_element_type=f32
    ).astype(bf16)
    return (after_ffn.astype(bf16), next_projection)


def solution(mesh):
    in_specs = (
        P("pool", "head"),
        P("pool", None, "head"),
        P("pool", None, None, "head"),
        P(),
        P(),
        P("pool", None),
        P("head", None),
        P(),
        P(),
        P(),
        P("pool", "head", None, None),
        P("pool", None, "head"),
        P(None, "head", None, None),
        P(None, None, "head"),
        P(),
        P(None, "head"),
    )
    out_specs = (P("pool", None), P("pool", "head"))
    return jax.shard_map(
        per_device, mesh=mesh, in_specs=in_specs, out_specs=out_specs, check_vma=False
    )
```

```python
import functools
import math

import jax
import jax.numpy as jnp
from jax import lax
from jax.experimental import pallas as pl
from jax.experimental.pallas import tpu as pltpu
from jax.sharding import PartitionSpec as P

HD = 128
LANES = 128
TILE = 16
MOST = 2
SPLIT = 4


epsilon = 1e-06
floor_score = -1e30
bf16 = jnp.bfloat16
f32 = jnp.float32
over_rows = (((0,), (0,)), ((), ()))
VMEM = pl.BlockSpec(memory_space=pltpu.VMEM)
FAR = pl.BlockSpec(memory_space=pltpu.HBM)


def iota(shape, dim):
    return lax.broadcasted_iota(jnp.int32, shape, dim)


def one_hot(mask):
    return mask.astype(f32).astype(bf16)


def dot(left, right):
    return jnp.dot(left, right, preferred_element_type=f32)


def call(kernel, name, outs, args, scratch=(), copies=(), far=(), megabytes=4, moved=1e5):
    semaphores = [pltpu.SemaphoreType.DMA((count,)) for count in copies]
    return pl.pallas_call(
        kernel,
        out_shape=[jax.ShapeDtypeStruct(shape, dtype) for shape, dtype in outs],
        in_specs=[FAR if i in far else VMEM for i in range(len(args))],
        out_specs=[VMEM] * len(outs),
        scratch_shapes=[pltpu.VMEM(shape, dtype) for shape, dtype in scratch] + semaphores,
        compiler_params=pltpu.CompilerParams(vmem_limit_bytes=int(megabytes * 2**20)),
        cost_estimate=pl.CostEstimate(
            flops=1000, bytes_accessed=int(moved), transcendentals=0
        ),
        name=name,
    )(*args)


def swap(value, axis, distance):
    count = lax.axis_size(axis)
    return lax.ppermute(value, axis, [(i, i ^ distance) for i in range(count)])


def start_weights(distance, slots, weight_ref, out_ref, semaphores):
    count, depth = out_ref.shape[:2]
    part = weight_ref.shape[0] * slots // lax.axis_size("head")
    first = (lax.axis_index("head") ^ distance) * part // slots
    rows = depth // SPLIT
    copies = [
        pltpu.make_async_copy(
            weight_ref.at[first + i, pl.ds(k * rows, rows)],
            out_ref.at[i, pl.ds(k * rows, rows)],
            semaphores.at[i * SPLIT + k],
        )
        for i in range(count)
        for k in range(SPLIT)
    ]
    for copy in copies:
        copy.start()
    return copies


def start_all_weights(distances, slots, weight_ref, out_refs, semaphores):
    copies = []
    for place, (distance, out_ref) in enumerate(zip(distances, out_refs)):
        count = out_ref.shape[0] * SPLIT
        own = semaphores.at[pl.ds(place * count, count)]
        copies += start_weights(distance, slots, weight_ref, out_ref, own)
    return copies


def setup_kernel(
    table_ref,
    length_ref,
    given_query_ref,
    given_fresh_ref,
    given_residual_ref,
    cache_ref,
    bias_ref,
    query_ref,
    fresh_ref,
    residual_ref,
):
    query_ref[...] = given_query_ref[...]
    fresh_ref[...] = given_fresh_ref[...]
    lane_width = residual_ref.shape[1]
    start = pl.multiple_of(lax.axis_index("head") * lane_width, LANES)
    residual_ref[...] = given_residual_ref[:, pl.ds(start, lane_width)]
    pool_idx = lax.axis_index("pool")
    blocks, _, block_len, _ = cache_ref.shape
    list_len, req_total = table_ref.shape
    tokens = blocks * block_len
    table = table_ref[...] - pool_idx * blocks
    left = length_ref[...] - iota((list_len, req_total), 0) * block_len
    block_row = iota((LANES, req_total), 0)
    limits = jnp.zeros((LANES, req_total), f32)
    for block in range(blocks):
        found = jnp.sum(jnp.where(table == block, left, 0).astype(f32), axis=0, keepdims=True)
        limits = jnp.where(block_row == block, found, limits)
    limits = jnp.clip(limits, 0.0, float(block_len)).astype(bf16)
    expand = iota((LANES, tokens), 1) // block_len == iota((LANES, tokens), 0)
    limits = lax.dot_general(limits, one_hot(expand), over_rows, preferred_element_type=f32)
    within = lax.rem(iota((1, tokens), 1), block_len).astype(f32)
    bias_ref[...] = jnp.where(within < limits, 0.0, floor_score)


def attention_kernel(
    order,
    cache_ref,
    bias_ref,
    fresh_ref,
    residual_ref,
    *refs,
):
    *query_refs, out_ref, queries_ref = refs
    blocks, _, block_len, _ = cache_ref.shape
    pool_idx = lax.axis_index("pool")
    pools, req_dev, lane_width = queries_ref.shape
    req_total = pools * req_dev
    tokens = blocks * block_len
    scale = 1.0 / math.sqrt(HD)
    bias = bias_ref[...]
    pieces = [ref[i] for ref in query_refs for i in range(ref.shape[0])]
    for distance, piece in zip(order, pieces):
        queries_ref[pool_idx ^ distance] = piece.astype(f32)
    queries = jnp.concatenate([queries_ref[i] for i in range(pools)], axis=0).astype(bf16)
    own = iota((req_total, req_dev), 0) == iota((req_total, req_dev), 1) + pool_idx * req_dev
    lane = iota((req_total, LANES), 1)
    side = jnp.zeros((req_total, LANES), f32)
    heads = lane_width // HD
    contract = (((1,), (1,)), ((), ()))
    for head in range(heads):
        columns = slice(head * HD, (head + 1) * HD)
        query = queries[:, columns]
        keys = cache_ref[:, 0, :, columns].reshape(tokens, HD)
        scores = lax.dot_general(query, keys, contract, preferred_element_type=f32) * scale
        scores = jnp.where(bias < 0.0, floor_score, scores)
        new_scores = (
            lax.dot_general(query, fresh_ref[:, 0, columns], contract, preferred_element_type=f32)
            * scale
        )
        new_scores = jnp.where(own, new_scores, floor_score)
        top = jnp.maximum(
            jnp.max(scores, axis=1, keepdims=True), jnp.max(new_scores, axis=1, keepdims=True)
        )
        top = top.astype(bf16).astype(f32)
        weights = jnp.where(bias < 0.0, 0.0, jnp.exp(scores - top))
        new_weights = jnp.where(own, jnp.exp(new_scores - top), 0.0)
        total = jnp.sum(weights, axis=1, keepdims=True) + jnp.sum(
            new_weights, axis=1, keepdims=True
        )
        values = cache_ref[:, 1, :, columns].reshape(tokens, HD)
        mixed = dot(weights.astype(bf16), values) + dot(
            new_weights.astype(bf16), fresh_ref[:, 1, columns]
        )
        inverse = jnp.where(total > 0.0, 1.0 / jnp.where(total > 0.0, total, 1.0), 0.0)
        out_ref[:req_total, columns] = (mixed * inverse).astype(bf16)
        coarse = total.astype(bf16).astype(f32)
        side = jnp.where(lane == head, top, side)
        side = jnp.where(lane == heads + head, coarse, side)
        side = jnp.where(lane == 2 * heads + head, total - coarse, side)
    out_ref[:req_total, lane_width:] = side.astype(bf16)
    out_ref[req_total:, :] = jnp.zeros((out_ref.shape[0] - req_total, out_ref.shape[1]), bf16)
    out_ref[req_total : req_total + req_dev, :lane_width] = residual_ref[...]


def merge_kernel(req_dev, parts_ref, weight_ref, *refs):
    out_refs, attended_ref = refs[:-1], refs[-1]
    count, _, packed = parts_ref.shape
    req_total, col_part = out_refs[0].shape
    lane_width = packed - LANES
    heads = lane_width // HD
    me = lax.axis_index("head")
    lane = iota((req_total, LANES), 1)
    sides = [parts_ref[i, :req_total, lane_width:].astype(f32) for i in range(count)]

    def column(side, place):
        return jnp.sum(jnp.where(lane == place, side, 0.0), axis=1, keepdims=True)

    for head in range(heads):
        columns = slice(head * HD, (head + 1) * HD)
        tops = [column(side, head) for side in sides]
        totals = [column(side, heads + head) + column(side, 2 * heads + head) for side in sides]
        top = functools.reduce(jnp.maximum, tops)
        shares = [total * jnp.exp(part - top) for part, total in zip(tops, totals)]
        denominator = functools.reduce(jnp.add, shares)
        mixed = functools.reduce(
            jnp.add,
            [shares[i] * parts_ref[i, :req_total, columns].astype(f32) for i in range(count)],
        )
        attended_ref[:, columns] = (mixed / denominator).astype(bf16)
    for distance, out_ref in enumerate(out_refs):
        start = pl.multiple_of((me ^ distance) * col_part, LANES)
        projected = dot(attended_ref[...], weight_ref[:, pl.ds(start, col_part)])
        out_ref[...] = projected.astype(out_ref.dtype)
    for i in range(count):
        rows = slice(i * req_dev, (i + 1) * req_dev)
        residual = parts_ref[i, req_total : req_total + req_dev, :col_part].astype(f32)
        out_refs[0][rows, :] = out_refs[0][rows, :] + residual


def routing_kernel(
    distances,
    slots,
    req_dev,
    routes_ref,
    gates_ref,
    far_weight_ref,
    pick_ref,
    coarse_ref,
    fine_ref,
    spread_ref,
    *refs,
):
    weight_refs, semaphores = refs[:-1], refs[-1]
    fetched = start_all_weights(distances, slots, far_weight_ref, weight_refs, semaphores)
    top_k, req_total = routes_ref.shape
    slot_total = coarse_ref.shape[0]
    extra = pick_ref.shape[0] - slot_total
    pool_idx = lax.axis_index("pool")
    expert = iota((slot_total, req_total), 0) // slots + pool_idx * (slot_total // slots)
    rank = lax.rem(iota((slot_total, req_total), 0), slots).astype(f32)
    chosen = jnp.zeros((slot_total, req_total), f32)
    gate = jnp.zeros((slot_total, req_total), f32)
    for k in range(top_k):
        match = routes_ref[k : k + 1, :] == expert
        chosen = jnp.where(match, 1.0, chosen)
        gate = jnp.where(match, gates_ref[k : k + 1, :], gate)
    earlier = iota((req_total, req_total), 0) < iota((req_total, req_total), 1)
    place = dot(chosen.astype(bf16), one_hot(earlier))
    pick = jnp.where(place == rank, chosen, 0.0)
    pick_ref[:slot_total, :] = pick.astype(bf16)
    own_place = iota((extra, req_total), 0)
    own = iota((extra, req_total), 1) == own_place + pool_idx * req_dev
    pick_ref[slot_total:, :] = one_hot(jnp.logical_and(own, own_place < req_dev))
    gate = gate * pick
    coarse = gate.astype(bf16)
    coarse_ref[...] = coarse
    fine_ref[...] = (gate - coarse.astype(f32)).astype(bf16)
    spread_ref[...] = one_hot(iota(spread_ref.shape, 1) == 2 * iota(spread_ref.shape, 0))
    for copy in fetched:
        copy.wait()


def gain_columns(gain_ref, part, count):
    gains = gain_ref[...].astype(f32)
    rows = iota(gains.shape, 0)
    first = part * (count // LANES)
    return jnp.concatenate(
        [
            jnp.sum(jnp.where(rows == first + i, gains, 0.0), axis=0, keepdims=True)
            for i in range(count // LANES)
        ],
        axis=1,
    )


def prepare_kernel(req_dev, gain_ref, pick_ref, spread_ref, own_sum_ref, *refs):
    received, (gate_ref, up_ref, side_ref, after_ref, all_ref) = refs[:-5], refs[-5:]
    req_total, col_part = own_sum_ref.shape
    after = own_sum_ref[...]
    for part in received:
        after = after + part[...].astype(f32)
    for place in range(all_ref.shape[0]):
        all_ref[place] = after[place * req_dev : (place + 1) * req_dev]
    after_ref[...] = all_ref[lax.axis_index("pool")]
    gains = gain_columns(gain_ref, lax.axis_index("head"), col_part)
    scaled = (after * gains).astype(bf16)
    squares = jnp.sum(after * after, axis=1, keepdims=True)
    coarse = squares.astype(bf16).astype(f32)
    lane = iota((req_total, LANES), 1)
    side = jnp.where(lane == 0, coarse, jnp.where(lane == 1, squares - coarse, 0.0))
    pick = pick_ref[...]
    picked = dot(pick, scaled).astype(bf16)
    side_ref[...] = dot(pick, side.astype(bf16)).astype(bf16)
    spread = dot(picked, spread_ref[...])
    gate_ref[...] = spread.astype(bf16)
    up_ref[...] = pltpu.roll(spread, 1, 1).astype(bf16)


def gate_up(lhs, weight, out_ref, rows, side):
    count, ffe = lhs.shape[0] // 2, weight.shape[1]
    sums = dot(lhs, weight)
    out_ref[rows, :ffe] = sums[:count].astype(out_ref.dtype)
    out_ref[rows, ffe : 2 * ffe] = sums[count:].astype(out_ref.dtype)
    out_ref[rows, 2 * ffe :] = side.astype(out_ref.dtype)


def expert_kernel(distance, slots, gate_ref, up_ref, side_ref, weight_ref, *refs):
    refs = list(refs)
    head_devs = lax.axis_size("head")
    if distance == 0:
        near_ref, semaphores = refs[-2:]
        refs = refs[:-2]
        fetched = start_weights(distance, slots, weight_ref, near_ref, semaphores)
        weight_ref = near_ref
        for copy in fetched:
            copy.wait()
    _, depth, _, ffe = weight_ref.shape
    target = lax.axis_index("head") ^ distance
    if distance == head_devs - 1:
        shared_weight_ref, out_ref, shared_ref, all_ref = refs
        extra, share = all_ref.shape[0], shared_ref.shape[1]
        first_extra = gate_ref.shape[0] - extra
        lhs = jnp.concatenate([gate_ref[first_extra:, :], up_ref[first_extra:, :]], axis=0)
        gate_up(
            lhs,
            shared_weight_ref[0].reshape(2 * depth, ffe),
            all_ref,
            slice(0, extra),
            side_ref[first_extra:, :],
        )
        for place in range(head_devs):
            shared_ref[place] = all_ref[place * share : (place + 1) * share, :]
    else:
        shared_ref, out_ref = refs[0], refs[-1]
        share = shared_ref.shape[1]
    part = out_ref.shape[0] - share
    each = min(slots, part)
    for i in range(part // each):
        rows = pl.ds(pl.multiple_of(target * part + i * each, TILE), each)
        lhs = jnp.concatenate([gate_ref[rows, :], up_ref[rows, :]], axis=0)
        weight = weight_ref[i].reshape(2 * depth, ffe)
        gate_up(lhs, weight, out_ref, slice(i * each, (i + 1) * each), side_ref[rows, :])
    out_ref[part:, :] = shared_ref[target].astype(bf16)


def add_kernel(own_ref, received_ref, out_ref):
    out_ref[...] = (own_ref[...].astype(f32) + received_ref[...].astype(f32)).astype(bf16)


def hidden_kernel(width, *refs):
    parts, out_ref = refs[:-1], refs[-1]
    ffe = out_ref.shape[1]

    def total(columns):
        return functools.reduce(jnp.add, [part[:, columns].astype(f32) for part in parts])

    side = total(slice(2 * ffe, 2 * ffe + LANES))
    row_scale = lax.rsqrt((side[:, 0:1] + side[:, 1:2]) / width + epsilon)
    gates = total(slice(0, ffe)) * row_scale
    ups = total(slice(ffe, 2 * ffe)) * row_scale
    out_ref[...] = (gates / (1.0 + jnp.exp(-gates)) * ups).astype(bf16)


def down_rows(distance, slots, hidden_ref, weight_ref):
    part = weight_ref.shape[0] * slots // lax.axis_size("head")
    each = min(slots, part)
    first = (lax.axis_index("head") ^ distance) * part
    return [
        dot(hidden_ref[i * each : (i + 1) * each, :], weight_ref[(first + i * each) // slots])
        for i in range(part // each)
    ]


def down_kernel(distance, slots, hidden_ref, weight_ref, out_ref):
    out_ref[...] = jnp.concatenate(down_rows(distance, slots, hidden_ref, weight_ref), axis=0)


def combine_kernel(distance, slots, coarse_ref, fine_ref, weight_ref, shared_weight_ref, *refs):
    head_devs = lax.axis_size("head")
    hidden_refs, done_refs = refs[:head_devs], refs[head_devs : 2 * head_devs - 1]
    routed_ref, shared_ref, rows_ref = refs[2 * head_devs - 1 :]
    me = lax.axis_index("head")
    part = weight_ref.shape[0] * slots // head_devs
    last = jnp.concatenate(
        down_rows(distance, slots, hidden_refs[distance], weight_ref), axis=0
    )
    done = {j: ref for j, ref in zip([j for j in range(head_devs) if j != distance], done_refs)}
    for j in range(head_devs):
        rows = pl.ds(pl.multiple_of((me ^ j) * part, TILE), part)
        rows_ref[rows, :] = last if j == distance else done[j][...]
    values = rows_ref[...]
    coarse = values.astype(bf16)
    fine = (values - coarse.astype(f32)).astype(bf16)
    def weighted(gates, rows):
        return lax.dot_general(gates, rows, over_rows, preferred_element_type=f32)

    gates = coarse_ref[...]
    routed = weighted(gates, coarse) + (weighted(gates, fine) + weighted(fine_ref[...], coarse))
    pools, req_dev, _ = routed_ref.shape
    for place in range(pools):
        routed_ref[place] = routed[place * req_dev : (place + 1) * req_dev].astype(bf16)
    share = shared_ref.shape[1]
    shared = jnp.concatenate([ref[part:, :].astype(f32) for ref in hidden_refs], axis=0)
    shared = dot(shared.astype(bf16), shared_weight_ref[0])
    for j in range(head_devs):
        shared_ref[me ^ j] = shared[j * share : (j + 1) * share]


def block_kernel(pieces_ref, shared_ref, after_ref, out_ref):
    req_dev = after_ref.shape[0]
    shared = jnp.concatenate([shared_ref[i] for i in range(shared_ref.shape[0])], axis=0)
    total = after_ref[...] + shared[:req_dev]
    for place in range(pieces_ref.shape[0]):
        total = total + pieces_ref[place].astype(f32)
    out_ref[...] = total.astype(bf16)


def join_kernel(*refs):
    place = 0
    for ref in refs[:-1]:
        count = ref.shape[0]
        refs[-1][place : place + count] = ref[...]
        place += count


def project_kernel(gain_ref, weight_ref, *refs):
    block_refs, (hidden_ref, out_ref) = refs[:-2], refs[-2:]
    me = lax.axis_index("head")
    blocks = [ref[...].astype(f32) for ref in block_refs]
    req_dev, col_part = blocks[0].shape
    width = hidden_ref.shape[1]
    squares = [jnp.sum(block * block, axis=1, keepdims=True) for block in blocks]
    row_scale = lax.rsqrt(functools.reduce(jnp.add, squares) / width + epsilon)
    total = jnp.zeros(out_ref.shape, f32)
    for distance, block in enumerate(blocks):
        start = pl.multiple_of((me ^ distance) * col_part, LANES)
        columns = pl.ds(start, col_part)
        hidden_ref[:, columns] = block.astype(bf16)
        gains = gain_columns(gain_ref, me ^ distance, col_part)
        normed = (block * row_scale * gains).astype(bf16)
        total = total + dot(normed, weight_ref[columns, :])
    out_ref[...] = total.astype(bf16)


def per_device(
    queries,
    fresh_pair,
    cache_blocks,
    block_table,
    lengths,
    residual,
    w_output,
    norm_gain,
    routes,
    route_gates,
    w_gate_up,
    w_down,
    shared_gate_up,
    shared_down,
    next_gain,
    w_query_key_value,
):
    pools = lax.axis_size("pool")
    head_devs = lax.axis_size("head")
    req_dev, lane_width = queries.shape
    req_total = block_table.shape[0]
    blk_count, _, block_len, _ = cache_blocks.shape
    exp_dev, col_part, _, ffe = w_gate_up.shape
    width = residual.shape[1]
    slots = min(MOST * pools, req_total)
    slot_total = exp_dev * slots
    extra = -(-req_dev // TILE) * TILE
    padded = -(-req_dev // TILE) * TILE + req_total
    small = pools <= 8
    distances = list(range(1, head_devs))
    piece_experts = max(1, exp_dev // head_devs)
    fetch_shape = ((piece_experts, col_part, 2, ffe), bf16)
    fetched = list(reversed(range(1, head_devs)))

    queries = queries[None]
    bias, own_queries, fresh, residual_part = call(
        setup_kernel,
        "setup",
        [
            ((req_total, blk_count * block_len), f32),
            (queries.shape, bf16),
            (fresh_pair.shape, bf16),
            ((req_dev, col_part), bf16),
        ],
        [block_table.T, lengths[None, :], queries, fresh_pair, residual, cache_blocks],
        megabytes=4 + 16 * req_total * blk_count * block_len / 2**20,
    )
    if small:
        order = list(range(0, pools, 2))
        pieces = [own_queries] + [swap(queries, "pool", d) for d in order[1:]]
        (joined,) = call(
            join_kernel, "join_queries", [((len(order), req_dev, lane_width), bf16)], pieces
        )
        pieces = [joined, swap(joined, "pool", 1)]
        order = order + [d + 1 for d in order]
    else:
        step = 1
        order, pieces = [0], [queries]
        while step < pools:
            whole = queries if step == 1 else jnp.concatenate(pieces, axis=0)
            pieces.append(swap(whole, "pool", step))
            order += [d ^ step for d in order]
            step *= 2
    (partial,) = call(
        functools.partial(attention_kernel, order),
        "attention",
        [((padded, lane_width + LANES), bf16)],
        [cache_blocks, bias, fresh, residual_part] + pieces,
        scratch=[((pools, req_dev, lane_width), f32)],
        megabytes=4 + 32 * req_total * blk_count * block_len / 2**20,
    )
    parts = lax.all_gather(partial, "pool", axis=0)
    sums = call(
        functools.partial(merge_kernel, req_dev),
        "merge_project",
        [((req_total, col_part), f32)] + [((req_total, col_part), bf16)] * (head_devs - 1),
        [parts, w_output],
        scratch=[((req_total, lane_width), bf16)],
        megabytes=5 + 12 * pools * req_total * LANES / 2**20,
    )
    pick, gate_coarse, gate_fine, spread, *weights = call(
        functools.partial(routing_kernel, fetched, slots, req_dev),
        "routing",
        [
            ((slot_total + extra, req_total), bf16),
            ((slot_total, req_total), bf16),
            ((slot_total, req_total), bf16),
            ((col_part, 2 * col_part), bf16),
        ]
        + [fetch_shape] * len(fetched),
        [routes.T, route_gates.T, w_gate_up],
        far=[2],
        copies=[len(fetched) * piece_experts * SPLIT],
        megabytes=24,
        moved=2e7,
    )
    weights = dict(zip(fetched, weights))
    received = {d: swap(sums[d], "head", d) for d in reversed(distances)}
    gate_rows, up_rows, side, own_after = call(
        functools.partial(prepare_kernel, req_dev),
        "prepare",
        [
            ((slot_total + extra, 2 * col_part), bf16),
            ((slot_total + extra, 2 * col_part), bf16),
            ((slot_total + extra, LANES), bf16),
            ((req_dev, col_part), f32),
        ],
        [norm_gain.reshape(-1, LANES), pick, spread, sums[0]] + [received[d] for d in distances],
        scratch=[((pools, req_dev, col_part), f32)],
        megabytes=6,
    )

    piece = slot_total // head_devs + extra // head_devs
    piece_shape = ((piece, 2 * ffe + LANES), bf16)
    shared_shape = ((head_devs, extra // head_devs, 2 * ffe + LANES), f32)
    shared_rows = None
    last = head_devs - 1

    def experts(distance, after=()):
        nonlocal shared_rows
        args = [gate_rows, up_rows, side, weights.get(distance, w_gate_up)]
        outs, scratch, copies, far = [piece_shape], [], [], []
        if distance == last:
            args, outs = args + [shared_gate_up], outs + [shared_shape]
            scratch = [((extra, 2 * ffe + LANES), f32)]
        else:
            args = args + [shared_rows] + list(after)
        if distance == 0:
            scratch, copies, far = [fetch_shape], [piece_experts * SPLIT], [3]
        mine, *shared = call(
            functools.partial(expert_kernel, distance, slots),
            f"experts_{distance}",
            outs,
            args,
            scratch=scratch,
            copies=copies,
            far=far,
            megabytes=32 if distance == 0 else 10,
        )
        if shared:
            (shared_rows,) = shared
        return mine

    if head_devs == 4:
        near = swap(experts(3), "head", 1)
        own_near = experts(1)
        near_own = swap(own_near, "head", 1)
        (pair,) = call(add_kernel, "add_pair", [piece_shape], [experts(2, [own_near]), near])
        parts = [experts(0, [pair]), swap(pair, "head", 2), near_own]
    else:
        parts = [swap(experts(d), "head", d) for d in reversed(range(1, head_devs))]
        parts = [experts(0)] + parts
    (hidden,) = call(
        functools.partial(hidden_kernel, width), "hidden", [((piece, ffe), bf16)], parts
    )
    hiddens = {0: hidden}
    for d in distances:
        hiddens[d] = swap(hidden, "head", d)
    done = []
    for d in range(last):
        done += call(
            functools.partial(down_kernel, d, slots),
            f"down_{d}",
            [((slot_total // head_devs, col_part), f32)],
            [hiddens[d], w_down],
            megabytes=6,
            )
    routed, shared_out = call(
        functools.partial(combine_kernel, last, slots),
        "combine",
        [((pools, req_dev, col_part), bf16), ((head_devs, extra // head_devs, col_part), f32)],
        [gate_coarse, gate_fine, w_down, shared_down]
        + [hiddens[d] for d in range(head_devs)]
        + done,
        scratch=[((slot_total, col_part), f32)],
        megabytes=6,
    )
    pieces = lax.all_to_all(routed, "pool", 0, 0)
    (block,) = call(
        block_kernel,
        "block",
        [((req_dev, col_part), bf16)],
        [pieces, shared_out, own_after],
        megabytes=4,
    )
    blocks = [block] + [swap(block, "head", d) for d in distances]
    next_hidden, next_projection = call(
        project_kernel,
        "project",
        [((req_dev, width), bf16), ((req_dev, w_query_key_value.shape[1]), bf16)],
        [next_gain.reshape(-1, LANES), w_query_key_value] + blocks,
        megabytes=6,
    )
    return (next_hidden, next_projection)


def solution(mesh):
    in_specs = (
        P("pool", "head"),
        P("pool", None, "head"),
        P("pool", None, None, "head"),
        P(),
        P(),
        P("pool", None),
        P("head", None),
        P(),
        P(),
        P(),
        P("pool", "head", None, None),
        P("pool", None, "head"),
        P(None, "head", None, None),
        P(None, None, "head"),
        P(),
        P(None, "head"),
    )
    out_specs = (P("pool", None), P("pool", "head"))
    return jax.shard_map(
        per_device, mesh=mesh, in_specs=in_specs, out_specs=out_specs, check_vma=False
    )
```

```python
import functools
import math

import jax
import jax.numpy as jnp
from jax import lax
from jax.experimental import pallas as pl
from jax.experimental.pallas import tpu as pltpu
from jax.sharding import PartitionSpec as P

HD = 128
LANES = 128
TILE = 16
MOST = 2
SPLIT = 4
HALF = LANES // 2


epsilon = 1e-06
floor_score = -1e30
bf16 = jnp.bfloat16
f32 = jnp.float32
over_rows = (((0,), (0,)), ((), ()))
VMEM = pl.BlockSpec(memory_space=pltpu.VMEM)
SMEM = pl.BlockSpec(memory_space=pltpu.SMEM)
FAR = pl.BlockSpec(memory_space=pltpu.HBM)


def iota(shape, dim):
    return lax.broadcasted_iota(jnp.int32, shape, dim)


def one_hot(mask):
    return mask.astype(f32).astype(bf16)


def dot(left, right):
    return jnp.dot(left, right, preferred_element_type=f32)


def place(shape):
    return SMEM if shape == (1,) else VMEM


def call(kernel, name, outs, args, scratch=(), copies=(), far=(), megabytes=4, moved=1e5):
    semaphores = [pltpu.SemaphoreType.DMA((count,)) for count in copies]
    return pl.pallas_call(
        kernel,
        out_shape=[jax.ShapeDtypeStruct(shape, dtype) for shape, dtype in outs],
        in_specs=[FAR if i in far else place(arg.shape) for i, arg in enumerate(args)],
        out_specs=[place(shape) for shape, _ in outs],
        scratch_shapes=[pltpu.VMEM(shape, dtype) for shape, dtype in scratch] + semaphores,
        compiler_params=pltpu.CompilerParams(vmem_limit_bytes=int(megabytes * 2**20)),
        cost_estimate=pl.CostEstimate(
            flops=1000, bytes_accessed=int(moved), transcendentals=0
        ),
        name=name,
    )(*args)


def swap(value, axis, distance):
    count = lax.axis_size(axis)
    return lax.ppermute(value, axis, [(i, i ^ distance) for i in range(count)])


def start_weights(distance, slots, weight_ref, out_ref, semaphores):
    count, depth = out_ref.shape[:2]
    part = weight_ref.shape[0] * slots // lax.axis_size("head")
    first = (lax.axis_index("head") ^ distance) * part // slots
    rows = depth // SPLIT
    copies = [
        pltpu.make_async_copy(
            weight_ref.at[first + i, pl.ds(k * rows, rows)],
            out_ref.at[i, pl.ds(k * rows, rows)],
            semaphores.at[i * SPLIT + k],
        )
        for i in range(count)
        for k in range(SPLIT)
    ]
    for copy in copies:
        copy.start()
    return copies


def start_all_weights(distances, slots, weight_ref, out_refs, semaphores):
    copies = []
    for place, (distance, out_ref) in enumerate(zip(distances, out_refs)):
        count = out_ref.shape[0] * SPLIT
        own = semaphores.at[pl.ds(place * count, count)]
        copies += start_weights(distance, slots, weight_ref, out_ref, own)
    return copies


def early_kernel(*refs):
    refs[-1][0] = 0


def setup_kernel(blocks, block_len, early_ref, table_ref, length_ref, bias_ref):
    pool_idx = lax.axis_index("pool")
    list_len, req_total = table_ref.shape
    tokens = blocks * block_len
    table = table_ref[...] - pool_idx * blocks
    left = length_ref[...] - iota((list_len, req_total), 0) * block_len
    block_row = iota((LANES, req_total), 0)
    limits = jnp.zeros((LANES, req_total), f32)
    for block in range(blocks):
        found = jnp.sum(jnp.where(table == block, left, 0).astype(f32), axis=0, keepdims=True)
        limits = jnp.where(block_row == block, found, limits)
    limits = jnp.clip(limits, 0.0, float(block_len)).astype(bf16)
    expand = iota((LANES, tokens), 1) // block_len == iota((LANES, tokens), 0)
    limits = lax.dot_general(limits, one_hot(expand), over_rows, preferred_element_type=f32)
    within = lax.rem(iota((1, tokens), 1), block_len).astype(f32)
    bias_ref[...] = jnp.where(within < limits, 0.0, floor_score)


def attention_kernel(
    order,
    cache_ref,
    bias_ref,
    fresh_ref,
    residual_ref,
    *refs,
):
    *query_refs, out_ref, queries_ref = refs
    blocks, _, block_len, _ = cache_ref.shape
    pool_idx = lax.axis_index("pool")
    pools, req_dev, lane_width = queries_ref.shape
    req_total = pools * req_dev
    tokens = blocks * block_len
    scale = 1.0 / math.sqrt(HD)
    bias = bias_ref[...]
    pieces = [ref[i] for ref in query_refs for i in range(ref.shape[0])]
    for distance, piece in zip(order, pieces):
        queries_ref[pool_idx ^ distance] = piece.astype(f32)
    queries = jnp.concatenate([queries_ref[i] for i in range(pools)], axis=0).astype(bf16)
    own = iota((req_total, req_dev), 0) == iota((req_total, req_dev), 1) + pool_idx * req_dev
    lane = iota((req_total, LANES), 1)
    side = jnp.zeros((req_total, LANES), f32)
    heads = lane_width // HD
    contract = (((1,), (1,)), ((), ()))
    for head in range(heads):
        columns = slice(head * HD, (head + 1) * HD)
        query = queries[:, columns]
        keys = cache_ref[:, 0, :, columns].reshape(tokens, HD)
        scores = lax.dot_general(query, keys, contract, preferred_element_type=f32) * scale
        scores = jnp.where(bias < 0.0, floor_score, scores)
        new_scores = (
            lax.dot_general(query, fresh_ref[:, 0, columns], contract, preferred_element_type=f32)
            * scale
        )
        new_scores = jnp.where(own, new_scores, floor_score)
        top = jnp.maximum(
            jnp.max(scores, axis=1, keepdims=True), jnp.max(new_scores, axis=1, keepdims=True)
        )
        top = top.astype(bf16).astype(f32)
        weights = jnp.where(bias < 0.0, 0.0, jnp.exp(scores - top))
        new_weights = jnp.where(own, jnp.exp(new_scores - top), 0.0)
        total = jnp.sum(weights, axis=1, keepdims=True) + jnp.sum(
            new_weights, axis=1, keepdims=True
        )
        values = cache_ref[:, 1, :, columns].reshape(tokens, HD)
        mixed = dot(weights.astype(bf16), values) + dot(
            new_weights.astype(bf16), fresh_ref[:, 1, columns]
        )
        inverse = jnp.where(total > 0.0, 1.0 / jnp.where(total > 0.0, total, 1.0), 0.0)
        out_ref[:, columns] = (mixed * inverse).astype(bf16)
        coarse = total.astype(bf16).astype(f32)
        side = jnp.where(lane == head, top, side)
        side = jnp.where(lane == heads + head, coarse, side)
        side = jnp.where(lane == 2 * heads + head, total - coarse, side)
    out_ref[:, lane_width:] = side.astype(bf16)
    start = pl.multiple_of(lax.axis_index("head") * lane_width, LANES)
    residual = residual_ref[:, pl.ds(start, lane_width)]
    for i in range(lane_width // HALF):
        rows = slice(i * req_dev, (i + 1) * req_dev)
        out_ref[rows, lane_width + HALF :] = residual[:, i * HALF : (i + 1) * HALF]


def merge_kernel(req_dev, parts_ref, weight_ref, *refs):
    out_refs, attended_ref = refs[:-1], refs[-1]
    count, req_total, packed = parts_ref.shape
    col_part = out_refs[0].shape[1]
    lane_width = packed - LANES
    heads = lane_width // HD
    me = lax.axis_index("head")
    lane = iota((req_total, LANES), 1)
    sides = [parts_ref[i, :, lane_width:].astype(f32) for i in range(count)]

    def column(side, place):
        return jnp.sum(jnp.where(lane == place, side, 0.0), axis=1, keepdims=True)

    for head in range(heads):
        columns = slice(head * HD, (head + 1) * HD)
        tops = [column(side, head) for side in sides]
        totals = [column(side, heads + head) + column(side, 2 * heads + head) for side in sides]
        top = functools.reduce(jnp.maximum, tops)
        shares = [total * jnp.exp(part - top) for part, total in zip(tops, totals)]
        denominator = functools.reduce(jnp.add, shares)
        mixed = functools.reduce(
            jnp.add,
            [shares[i] * parts_ref[i, :, columns].astype(f32) for i in range(count)],
        )
        attended_ref[:, columns] = (mixed / denominator).astype(bf16)
    for distance, out_ref in enumerate(out_refs):
        start = pl.multiple_of((me ^ distance) * col_part, LANES)
        projected = dot(attended_ref[...], weight_ref[:, pl.ds(start, col_part)])
        out_ref[...] = projected.astype(out_ref.dtype)
    for i, side in enumerate(sides):
        rows = slice(i * req_dev, (i + 1) * req_dev)
        pieces = [
            side[k * req_dev : (k + 1) * req_dev, HALF:] for k in range(lane_width // HALF)
        ]
        out_refs[0][rows, :] = out_refs[0][rows, :] + jnp.concatenate(pieces, axis=1)


def routing_kernel(
    distances,
    slots,
    req_dev,
    routes_ref,
    gates_ref,
    after_ref,
    far_weight_ref,
    pick_ref,
    coarse_ref,
    fine_ref,
    spread_ref,
    *refs,
):
    weight_refs, semaphores = refs[:-1], refs[-1]
    fetched = start_all_weights(distances, slots, far_weight_ref, weight_refs, semaphores)
    top_k, req_total = routes_ref.shape
    slot_total = coarse_ref.shape[0]
    extra = pick_ref.shape[0] - slot_total
    pool_idx = lax.axis_index("pool")
    expert = iota((slot_total, req_total), 0) // slots + pool_idx * (slot_total // slots)
    rank = lax.rem(iota((slot_total, req_total), 0), slots).astype(f32)
    chosen = jnp.zeros((slot_total, req_total), f32)
    gate = jnp.zeros((slot_total, req_total), f32)
    for k in range(top_k):
        match = routes_ref[k : k + 1, :] == expert
        chosen = jnp.where(match, 1.0, chosen)
        gate = jnp.where(match, gates_ref[k : k + 1, :], gate)
    earlier = iota((req_total, req_total), 0) < iota((req_total, req_total), 1)
    place = dot(chosen.astype(bf16), one_hot(earlier))
    pick = jnp.where(place == rank, chosen, 0.0)
    pick_ref[:slot_total, :] = pick.astype(bf16)
    own_place = iota((extra, req_total), 0)
    own = iota((extra, req_total), 1) == own_place + pool_idx * req_dev
    pick_ref[slot_total:, :] = one_hot(jnp.logical_and(own, own_place < req_dev))
    gate = gate * pick
    coarse = gate.astype(bf16)
    coarse_ref[...] = coarse
    fine_ref[...] = (gate - coarse.astype(f32)).astype(bf16)
    spread_ref[...] = one_hot(iota(spread_ref.shape, 1) == 2 * iota(spread_ref.shape, 0))
    for copy in fetched:
        copy.wait()


def gain_columns(gain_ref, part, count):
    gains = gain_ref[...].astype(f32)
    rows = iota(gains.shape, 0)
    first = part * (count // LANES)
    return jnp.concatenate(
        [
            jnp.sum(jnp.where(rows == first + i, gains, 0.0), axis=0, keepdims=True)
            for i in range(count // LANES)
        ],
        axis=1,
    )


def prepare_kernel(req_dev, gain_ref, pick_ref, spread_ref, own_sum_ref, *refs):
    received, (gate_ref, up_ref, side_ref, after_ref, all_ref) = refs[:-5], refs[-5:]
    req_total, col_part = own_sum_ref.shape
    after = own_sum_ref[...]
    for part in received:
        after = after + part[...].astype(f32)
    for place in range(all_ref.shape[0]):
        all_ref[place] = after[place * req_dev : (place + 1) * req_dev]
    after_ref[...] = all_ref[lax.axis_index("pool")]
    gains = gain_columns(gain_ref, lax.axis_index("head"), col_part)
    scaled = (after * gains).astype(bf16)
    squares = jnp.sum(after * after, axis=1, keepdims=True)
    coarse = squares.astype(bf16).astype(f32)
    lane = iota((req_total, LANES), 1)
    side = jnp.where(lane == 0, coarse, jnp.where(lane == 1, squares - coarse, 0.0))
    pick = pick_ref[...]
    picked = dot(pick, scaled).astype(bf16)
    side_ref[...] = dot(pick, side.astype(bf16)).astype(bf16)
    spread = dot(picked, spread_ref[...])
    gate_ref[...] = spread.astype(bf16)
    up_ref[...] = pltpu.roll(spread, 1, 1).astype(bf16)


def gate_up(lhs, weight, out_ref, rows, side):
    count, ffe = lhs.shape[0] // 2, weight.shape[1]
    sums = dot(lhs, weight)
    out_ref[rows, :ffe] = sums[:count].astype(out_ref.dtype)
    out_ref[rows, ffe : 2 * ffe] = sums[count:].astype(out_ref.dtype)
    out_ref[rows, 2 * ffe :] = side.astype(out_ref.dtype)


def expert_kernel(distance, slots, gate_ref, up_ref, side_ref, weight_ref, *refs):
    refs = list(refs)
    head_devs = lax.axis_size("head")
    if distance == 0:
        near_ref, semaphores = refs[-2:]
        refs = refs[:-2]
        fetched = start_weights(distance, slots, weight_ref, near_ref, semaphores)
        weight_ref = near_ref
        for copy in fetched:
            copy.wait()
    _, depth, _, ffe = weight_ref.shape
    target = lax.axis_index("head") ^ distance
    if distance == head_devs - 1:
        shared_weight_ref, out_ref, shared_ref, all_ref = refs
        extra, share = all_ref.shape[0], shared_ref.shape[1]
        first_extra = gate_ref.shape[0] - extra
        lhs = jnp.concatenate([gate_ref[first_extra:, :], up_ref[first_extra:, :]], axis=0)
        gate_up(
            lhs,
            shared_weight_ref[0].reshape(2 * depth, ffe),
            all_ref,
            slice(0, extra),
            side_ref[first_extra:, :],
        )
        for place in range(head_devs):
            shared_ref[place] = all_ref[place * share : (place + 1) * share, :]
    else:
        shared_ref, out_ref = refs[0], refs[-1]
        share = shared_ref.shape[1]
    part = out_ref.shape[0] - share
    each = min(slots, part)
    for i in range(part // each):
        rows = pl.ds(pl.multiple_of(target * part + i * each, TILE), each)
        lhs = jnp.concatenate([gate_ref[rows, :], up_ref[rows, :]], axis=0)
        weight = weight_ref[i].reshape(2 * depth, ffe)
        gate_up(lhs, weight, out_ref, slice(i * each, (i + 1) * each), side_ref[rows, :])
    out_ref[part:, :] = shared_ref[target].astype(bf16)


def add_kernel(own_ref, received_ref, later_ref, out_ref, sent_ref):
    out_ref[...] = (own_ref[...].astype(f32) + received_ref[...].astype(f32)).astype(bf16)
    sent_ref[...] = later_ref[...]


def hidden_kernel(width, *refs):
    parts, out_ref = refs[:-1], refs[-1]
    ffe = out_ref.shape[1]

    def total(columns):
        return functools.reduce(jnp.add, [part[:, columns].astype(f32) for part in parts])

    side = total(slice(2 * ffe, 2 * ffe + LANES))
    row_scale = lax.rsqrt((side[:, 0:1] + side[:, 1:2]) / width + epsilon)
    gates = total(slice(0, ffe)) * row_scale
    ups = total(slice(ffe, 2 * ffe)) * row_scale
    out_ref[...] = (gates / (1.0 + jnp.exp(-gates)) * ups).astype(bf16)


def down_rows(distance, slots, hidden_ref, weight_ref):
    part = weight_ref.shape[0] * slots // lax.axis_size("head")
    each = min(slots, part)
    first = (lax.axis_index("head") ^ distance) * part
    return [
        dot(hidden_ref[i * each : (i + 1) * each, :], weight_ref[(first + i * each) // slots])
        for i in range(part // each)
    ]


def down_kernel(distance, slots, hidden_ref, weight_ref, out_ref):
    out_ref[...] = jnp.concatenate(down_rows(distance, slots, hidden_ref, weight_ref), axis=0)


def combine_kernel(distance, slots, coarse_ref, fine_ref, weight_ref, shared_weight_ref, *refs):
    head_devs = lax.axis_size("head")
    hidden_refs, done_refs = refs[:head_devs], refs[head_devs : 2 * head_devs - 1]
    routed_ref, shared_ref, rows_ref = refs[2 * head_devs - 1 :]
    me = lax.axis_index("head")
    part = weight_ref.shape[0] * slots // head_devs
    last = jnp.concatenate(
        down_rows(distance, slots, hidden_refs[distance], weight_ref), axis=0
    )
    done = {j: ref for j, ref in zip([j for j in range(head_devs) if j != distance], done_refs)}
    for j in range(head_devs):
        rows = pl.ds(pl.multiple_of((me ^ j) * part, TILE), part)
        rows_ref[rows, :] = last if j == distance else done[j][...]
    values = rows_ref[...]
    coarse = values.astype(bf16)
    fine = (values - coarse.astype(f32)).astype(bf16)
    def weighted(gates, rows):
        return lax.dot_general(gates, rows, over_rows, preferred_element_type=f32)

    gates = coarse_ref[...]
    routed = weighted(gates, coarse) + (weighted(gates, fine) + weighted(fine_ref[...], coarse))
    pools, req_dev, _ = routed_ref.shape
    for place in range(pools):
        routed_ref[place] = routed[place * req_dev : (place + 1) * req_dev].astype(bf16)
    share = shared_ref.shape[1]
    shared = jnp.concatenate([ref[part:, :].astype(f32) for ref in hidden_refs], axis=0)
    shared = dot(shared.astype(bf16), shared_weight_ref[0])
    for j in range(head_devs):
        shared_ref[me ^ j] = shared[j * share : (j + 1) * share]


def block_kernel(pieces_ref, shared_ref, after_ref, out_ref):
    req_dev = after_ref.shape[0]
    shared = jnp.concatenate([shared_ref[i] for i in range(shared_ref.shape[0])], axis=0)
    total = after_ref[...] + shared[:req_dev]
    for place in range(pieces_ref.shape[0]):
        total = total + pieces_ref[place].astype(f32)
    out_ref[...] = total.astype(bf16)


def join_kernel(bias_ref, *refs):
    for place, ref in enumerate(refs[:-1]):
        refs[-1][place] = ref[0]


def project_kernel(distances, width, gain_ref, weight_ref, *refs):
    me = lax.axis_index("head")
    count = len(distances)
    block_refs, refs = refs[:count], refs[count:]
    if distances[0] == 0:
        total_ref, side_ref = refs
        total, squares = jnp.zeros(total_ref.shape, f32), 0.0
    else:
        own_ref, given_total_ref, given_side_ref, hidden_ref, out_ref = refs
        total, squares = given_total_ref[...], given_side_ref[:, 0:1]
    for distance, ref in zip(distances, block_refs):
        block = ref[...].astype(f32)
        req_dev, col_part = block.shape
        columns = pl.ds(pl.multiple_of((me ^ distance) * col_part, LANES), col_part)
        if distances[0] != 0:
            hidden_ref[:, columns] = ref[...]
        squares = squares + jnp.sum(block * block, axis=1, keepdims=True)
        scaled = (block * gain_columns(gain_ref, me ^ distance, col_part)).astype(bf16)
        total = total + dot(scaled, weight_ref[columns, :])
    if distances[0] == 0:
        total_ref[...] = total
        side_ref[...] = jnp.broadcast_to(squares, side_ref.shape)
    else:
        columns = pl.ds(pl.multiple_of(me * col_part, LANES), col_part)
        hidden_ref[:, columns] = own_ref[...]
        out_ref[...] = (total * lax.rsqrt(squares / width + epsilon)).astype(bf16)


def per_device(
    queries,
    fresh_pair,
    cache_blocks,
    block_table,
    lengths,
    residual,
    w_output,
    norm_gain,
    routes,
    route_gates,
    w_gate_up,
    w_down,
    shared_gate_up,
    shared_down,
    next_gain,
    w_query_key_value,
):
    pools = lax.axis_size("pool")
    head_devs = lax.axis_size("head")
    req_dev, lane_width = queries.shape
    req_total = block_table.shape[0]
    blk_count, _, block_len, _ = cache_blocks.shape
    exp_dev, col_part, _, ffe = w_gate_up.shape
    width = residual.shape[1]
    slots = min(MOST * pools, req_total)
    slot_total = exp_dev * slots
    extra = -(-req_dev // TILE) * TILE
    small = pools <= 8
    distances = list(range(1, head_devs))
    piece_experts = max(1, exp_dev // head_devs)
    fetch_shape = ((piece_experts, col_part, 2, ffe), bf16)
    fetched = list(reversed(range(1, head_devs)))

    queries = queries[None]
    table, counts = block_table.T, lengths[None, :]
    later = [queries, table, counts, cache_blocks, fresh_pair, residual, w_gate_up]
    (early,) = call(
        early_kernel,
        "early",
        [((1,), jnp.int32)],
        later,
        far=range(len(later)),
        megabytes=59,
    )
    (bias,) = call(
        functools.partial(setup_kernel, blk_count, block_len),
        "setup",
        [((req_total, blk_count * block_len), f32)],
        [early, table, counts],
        megabytes=4 + 16 * req_total * blk_count * block_len / 2**20,
    )
    if small:
        order = list(range(0, pools, 2))
        pieces = [queries] + [swap(queries, "pool", d) for d in order[1:]]
        (joined,) = call(
            join_kernel,
            "join_queries",
            [((len(order), req_dev, lane_width), bf16)],
            [bias] + pieces,
            far=[0],
        )
        pieces = [joined, swap(joined, "pool", 1)]
        order = order + [d + 1 for d in order]
    else:
        step = 1
        order, pieces = [0], [queries]
        while step < pools:
            whole = queries if step == 1 else jnp.concatenate(pieces, axis=0)
            pieces.append(swap(whole, "pool", step))
            order += [d ^ step for d in order]
            step *= 2
    (partial,) = call(
        functools.partial(attention_kernel, order),
        "attention",
        [((req_total, lane_width + LANES), bf16)],
        [cache_blocks, bias, fresh_pair, residual] + pieces,
        scratch=[((pools, req_dev, lane_width), f32)],
        megabytes=4 + 32 * req_total * blk_count * block_len / 2**20,
    )
    parts = lax.all_gather(partial, "pool", axis=0)
    sums = call(
        functools.partial(merge_kernel, req_dev),
        "merge_project",
        [((req_total, col_part), f32)] + [((req_total, col_part), bf16)] * (head_devs - 1),
        [parts, w_output],
        scratch=[((req_total, lane_width), bf16)],
        megabytes=5 + 12 * pools * req_total * LANES / 2**20,
    )
    pick, gate_coarse, gate_fine, spread, *weights = call(
        functools.partial(routing_kernel, fetched, slots, req_dev),
        "routing",
        [
            ((slot_total + extra, req_total), bf16),
            ((slot_total, req_total), bf16),
            ((slot_total, req_total), bf16),
            ((col_part, 2 * col_part), bf16),
        ]
        + [fetch_shape] * len(fetched),
        [routes.T, route_gates.T, sums[0], w_gate_up],
        far=[3],
        copies=[len(fetched) * piece_experts * SPLIT],
        megabytes=24,
        moved=2e7,
    )
    weights = dict(zip(fetched, weights))
    received = {d: swap(sums[d], "head", d) for d in reversed(distances)}
    gate_rows, up_rows, side, own_after = call(
        functools.partial(prepare_kernel, req_dev),
        "prepare",
        [
            ((slot_total + extra, 2 * col_part), bf16),
            ((slot_total + extra, 2 * col_part), bf16),
            ((slot_total + extra, LANES), bf16),
            ((req_dev, col_part), f32),
        ],
        [norm_gain.reshape(-1, LANES), pick, spread, sums[0]] + [received[d] for d in distances],
        scratch=[((pools, req_dev, col_part), f32)],
        megabytes=6,
    )

    piece = slot_total // head_devs + extra // head_devs
    piece_shape = ((piece, 2 * ffe + LANES), bf16)
    shared_shape = ((head_devs, extra // head_devs, 2 * ffe + LANES), f32)
    shared_rows = None
    last = head_devs - 1

    def experts(distance, after=()):
        nonlocal shared_rows
        args = [gate_rows, up_rows, side, weights.get(distance, w_gate_up)]
        outs, scratch, copies, far = [piece_shape], [], [], []
        if distance == last:
            args, outs = args + [shared_gate_up], outs + [shared_shape]
            scratch = [((extra, 2 * ffe + LANES), f32)]
        else:
            args = args + [shared_rows] + list(after)
        if distance == 0:
            scratch, copies, far = [fetch_shape], [piece_experts * SPLIT], [3]
        mine, *shared = call(
            functools.partial(expert_kernel, distance, slots),
            f"experts_{distance}",
            outs,
            args,
            scratch=scratch,
            copies=copies,
            far=far,
            megabytes=32 if distance == 0 else 10,
        )
        if shared:
            (shared_rows,) = shared
        return mine

    if head_devs == 4:
        near = swap(experts(3), "head", 1)
        own_near = experts(1)
        pair, own_near = call(
            add_kernel,
            "add_pair",
            [piece_shape, piece_shape],
            [experts(2, [own_near]), near, own_near],
        )
        far = swap(pair, "head", 2)
        parts = [experts(0, [pair]), far, swap(own_near, "head", 1)]
    else:
        parts = [swap(experts(d), "head", d) for d in reversed(range(1, head_devs))]
        parts = [experts(0)] + parts
    (hidden,) = call(
        functools.partial(hidden_kernel, width), "hidden", [((piece, ffe), bf16)], parts
    )
    hiddens = {0: hidden}
    for d in distances:
        hiddens[d] = swap(hidden, "head", d)
    done = []
    for d in range(last):
        done += call(
            functools.partial(down_kernel, d, slots),
            f"down_{d}",
            [((slot_total // head_devs, col_part), f32)],
            [hiddens[d], w_down],
            megabytes=6,
            )
    routed, shared_out = call(
        functools.partial(combine_kernel, last, slots),
        "combine",
        [((pools, req_dev, col_part), bf16), ((head_devs, extra // head_devs, col_part), f32)],
        [gate_coarse, gate_fine, w_down, shared_down]
        + [hiddens[d] for d in range(head_devs)]
        + done,
        scratch=[((slot_total, col_part), f32)],
        megabytes=6,
    )
    pieces = lax.all_to_all(routed, "pool", 0, 0)
    (block,) = call(
        block_kernel,
        "block",
        [((req_dev, col_part), bf16)],
        [pieces, shared_out, own_after],
        megabytes=4,
    )
    blocks = [block] + [swap(block, "head", d) for d in distances]
    last_args = [next_gain.reshape(-1, LANES), w_query_key_value]
    out_width = w_query_key_value.shape[1]
    total, squares = call(
        functools.partial(project_kernel, [0], width),
        "project_own",
        [((req_dev, out_width), f32), ((req_dev, LANES), f32)],
        last_args + [block],
        megabytes=6,
    )
    next_hidden, next_projection = call(
        functools.partial(project_kernel, distances, width),
        "project",
        [((req_dev, width), bf16), ((req_dev, out_width), bf16)],
        last_args + blocks[1:] + [block, total, squares],
        megabytes=6,
    )
    return (next_hidden, next_projection)


def solution(mesh):
    in_specs = (
        P("pool", "head"),
        P("pool", None, "head"),
        P("pool", None, None, "head"),
        P(),
        P(),
        P("pool", None),
        P("head", None),
        P(),
        P(),
        P(),
        P("pool", "head", None, None),
        P("pool", None, "head"),
        P(None, "head", None, None),
        P(None, None, "head"),
        P(),
        P(None, "head"),
    )
    out_specs = (P("pool", None), P("pool", "head"))
    return jax.shard_map(
        per_device, mesh=mesh, in_specs=in_specs, out_specs=out_specs, check_vma=False
    )
```

```python
import functools
import math

import jax
import jax.numpy as jnp
from jax import lax
from jax.experimental import pallas as pl
from jax.experimental.pallas import tpu as pltpu
from jax.sharding import PartitionSpec as P

HD = 128
LANES = 128
TILE = 16
MOST = 2
SPLIT = 4
HALF = LANES // 2


epsilon = 1e-06
floor_score = -1e30
least_score = -1e29
bf16 = jnp.bfloat16
f32 = jnp.float32
over_rows = (((0,), (0,)), ((), ()))
VMEM = pl.BlockSpec(memory_space=pltpu.VMEM)
SMEM = pl.BlockSpec(memory_space=pltpu.SMEM)
FAR = pl.BlockSpec(memory_space=pltpu.HBM)


def iota(shape, dim):
    return lax.broadcasted_iota(jnp.int32, shape, dim)


def one_hot(mask):
    return mask.astype(f32).astype(bf16)


def dot(left, right):
    return jnp.dot(left, right, preferred_element_type=f32)


def place(shape):
    return SMEM if shape == (1,) else VMEM


def call(kernel, name, outs, args, scratch=(), copies=(), far=(), megabytes=4, moved=1e5):
    semaphores = [pltpu.SemaphoreType.DMA((count,)) for count in copies]
    return pl.pallas_call(
        kernel,
        out_shape=[jax.ShapeDtypeStruct(shape, dtype) for shape, dtype in outs],
        in_specs=[FAR if i in far else place(arg.shape) for i, arg in enumerate(args)],
        out_specs=[place(shape) for shape, _ in outs],
        scratch_shapes=[pltpu.VMEM(shape, dtype) for shape, dtype in scratch] + semaphores,
        compiler_params=pltpu.CompilerParams(vmem_limit_bytes=int(megabytes * 2**20)),
        cost_estimate=pl.CostEstimate(
            flops=1000, bytes_accessed=int(moved), transcendentals=0
        ),
        name=name,
    )(*args)


def swap(value, axis, distance):
    count = lax.axis_size(axis)
    return lax.ppermute(value, axis, [(i, i ^ distance) for i in range(count)])


def start_weights(distance, slots, weight_ref, out_ref, semaphores):
    count, depth = out_ref.shape[:2]
    part = weight_ref.shape[0] * slots // lax.axis_size("head")
    first = (lax.axis_index("head") ^ distance) * part // slots
    rows = depth // SPLIT
    copies = [
        pltpu.make_async_copy(
            weight_ref.at[first + i, pl.ds(k * rows, rows)],
            out_ref.at[i, pl.ds(k * rows, rows)],
            semaphores.at[i * SPLIT + k],
        )
        for i in range(count)
        for k in range(SPLIT)
    ]
    for copy in copies:
        copy.start()
    return copies


def start_all_weights(distances, slots, weight_ref, out_refs, semaphores):
    copies = []
    for place, (distance, out_ref) in enumerate(zip(distances, out_refs)):
        count = out_ref.shape[0] * SPLIT
        own = semaphores.at[pl.ds(place * count, count)]
        copies += start_weights(distance, slots, weight_ref, out_ref, own)
    return copies


def early_kernel(*refs):
    refs[-1][0] = 0


def setup_kernel(blocks, block_len, early_ref, table_ref, length_ref, bias_ref):
    pool_idx = lax.axis_index("pool")
    list_len, req_total = table_ref.shape
    tokens = blocks * block_len
    table = table_ref[...] - pool_idx * blocks
    left = length_ref[...] - iota((list_len, req_total), 0) * block_len
    block_row = iota((LANES, req_total), 0)
    limits = jnp.zeros((LANES, req_total), f32)
    for block in range(blocks):
        found = jnp.sum(jnp.where(table == block, left, 0).astype(f32), axis=0, keepdims=True)
        limits = jnp.where(block_row == block, found, limits)
    limits = jnp.clip(limits, 0.0, float(block_len)).astype(bf16)
    expand = iota((LANES, tokens), 1) // block_len == iota((LANES, tokens), 0)
    limits = lax.dot_general(limits, one_hot(expand), over_rows, preferred_element_type=f32)
    within = lax.rem(iota((1, tokens), 1), block_len).astype(f32)
    bias_ref[...] = jnp.where(within < limits, 0.0, floor_score)


def attention_kernel(
    order,
    cache_ref,
    bias_ref,
    fresh_ref,
    residual_ref,
    *refs,
):
    *query_refs, out_ref, queries_ref = refs
    blocks, _, block_len, _ = cache_ref.shape
    pool_idx = lax.axis_index("pool")
    pools, req_dev, lane_width = queries_ref.shape
    req_total = pools * req_dev
    tokens = blocks * block_len
    scale = math.log2(math.e) / math.sqrt(HD)
    bias = bias_ref[...]
    pieces = [ref[i] for ref in query_refs for i in range(ref.shape[0])]
    for distance, piece in zip(order, pieces):
        queries_ref[pool_idx ^ distance] = piece.astype(f32)
    queries = jnp.concatenate([queries_ref[i] for i in range(pools)], axis=0).astype(bf16)
    own = iota((req_total, req_dev), 0) == iota((req_total, req_dev), 1) + pool_idx * req_dev
    own_bias = jnp.where(own, 0.0, floor_score)
    lane = iota((req_total, LANES), 1)
    side = jnp.zeros((req_total, LANES), f32)
    heads = lane_width // HD
    contract = (((1,), (1,)), ((), ()))
    for head in range(heads):
        columns = slice(head * HD, (head + 1) * HD)
        query = queries[:, columns]
        keys = cache_ref[:, 0, :, columns].reshape(tokens, HD)
        scores = lax.dot_general(query, keys, contract, preferred_element_type=f32) * scale + bias
        new_scores = (
            lax.dot_general(query, fresh_ref[:, 0, columns], contract, preferred_element_type=f32)
            * scale
            + own_bias
        )
        top = jnp.maximum(
            jnp.max(scores, axis=1, keepdims=True), jnp.max(new_scores, axis=1, keepdims=True)
        )
        top = jnp.maximum(top, least_score).astype(bf16).astype(f32)
        weights = jnp.exp2(scores - top)
        new_weights = jnp.exp2(new_scores - top)
        total = jnp.sum(weights, axis=1, keepdims=True) + jnp.sum(
            new_weights, axis=1, keepdims=True
        )
        values = cache_ref[:, 1, :, columns].reshape(tokens, HD)
        mixed = dot(weights.astype(bf16), values) + dot(
            new_weights.astype(bf16), fresh_ref[:, 1, columns]
        )
        inverse = jnp.where(total > 0.0, 1.0 / jnp.where(total > 0.0, total, 1.0), 0.0)
        out_ref[:, columns] = (mixed * inverse).astype(bf16)
        coarse = total.astype(bf16).astype(f32)
        side = jnp.where(lane == head, top, side)
        side = jnp.where(lane == heads + head, coarse, side)
        side = jnp.where(lane == 2 * heads + head, total - coarse, side)
    out_ref[:, lane_width:] = side.astype(bf16)
    start = pl.multiple_of(lax.axis_index("head") * lane_width, LANES)
    residual = residual_ref[:, pl.ds(start, lane_width)]
    for i in range(lane_width // HALF):
        rows = slice(i * req_dev, (i + 1) * req_dev)
        out_ref[rows, lane_width + HALF :] = residual[:, i * HALF : (i + 1) * HALF]


def merge_kernel(req_dev, parts_ref, weight_ref, *refs):
    out_refs, attended_ref = refs[:-1], refs[-1]
    count, req_total, packed = parts_ref.shape
    col_part = out_refs[0].shape[1]
    lane_width = packed - LANES
    heads = lane_width // HD
    me = lax.axis_index("head")
    sides = [parts_ref[i, :, lane_width:].astype(f32) for i in range(count)]
    lane = iota((req_total, LANES), 1)
    tops = [jnp.where(lane < heads, side, 0.0) for side in sides]
    top = functools.reduce(jnp.maximum, tops)

    def shifted(side, by):
        return pltpu.roll(side, LANES - by, 1)

    shares = [
        (shifted(side, heads) + shifted(side, 2 * heads)) * jnp.exp2(part - top)
        for side, part in zip(sides, tops)
    ]
    denominator = functools.reduce(jnp.add, shares)
    inverse = 1.0 / jnp.where(lane < heads, denominator, 1.0)
    spread = iota((2 * LANES, lane_width), 1) // HD == lax.rem(
        iota((2 * LANES, lane_width), 0), LANES
    )
    spread = one_hot(spread)
    mixed = jnp.zeros((req_total, lane_width), f32)
    for i, share in enumerate(shares):
        share = jnp.where(lane < heads, share * inverse, 0.0)
        coarse = share.astype(bf16)
        fine = (share - coarse.astype(f32)).astype(bf16)
        weight = dot(jnp.concatenate([coarse, fine], axis=1), spread)
        mixed = mixed + weight * parts_ref[i, :, :lane_width].astype(f32)
    attended_ref[...] = mixed.astype(bf16)
    for distance, out_ref in enumerate(out_refs):
        start = pl.multiple_of((me ^ distance) * col_part, LANES)
        projected = dot(attended_ref[...], weight_ref[:, pl.ds(start, col_part)])
        out_ref[...] = projected.astype(out_ref.dtype)
    for i, side in enumerate(sides):
        rows = slice(i * req_dev, (i + 1) * req_dev)
        pieces = [
            side[k * req_dev : (k + 1) * req_dev, HALF:] for k in range(lane_width // HALF)
        ]
        out_refs[0][rows, :] = out_refs[0][rows, :] + jnp.concatenate(pieces, axis=1)


def routing_kernel(
    distances,
    slots,
    req_dev,
    routes_ref,
    gates_ref,
    after_ref,
    far_weight_ref,
    pick_ref,
    coarse_ref,
    fine_ref,
    spread_ref,
    *refs,
):
    weight_refs, semaphores = refs[:-1], refs[-1]
    fetched = start_all_weights(distances, slots, far_weight_ref, weight_refs, semaphores)
    top_k, req_total = routes_ref.shape
    slot_total = coarse_ref.shape[0]
    extra = pick_ref.shape[0] - slot_total
    pool_idx = lax.axis_index("pool")
    expert = iota((slot_total, req_total), 0) // slots + pool_idx * (slot_total // slots)
    rank = lax.rem(iota((slot_total, req_total), 0), slots).astype(f32)
    chosen = jnp.zeros((slot_total, req_total), f32)
    gate = jnp.zeros((slot_total, req_total), f32)
    for k in range(top_k):
        match = routes_ref[k : k + 1, :] == expert
        chosen = jnp.where(match, 1.0, chosen)
        gate = jnp.where(match, gates_ref[k : k + 1, :], gate)
    earlier = iota((req_total, req_total), 0) < iota((req_total, req_total), 1)
    place = dot(chosen.astype(bf16), one_hot(earlier))
    pick = jnp.where(place == rank, chosen, 0.0)
    pick_ref[:slot_total, :] = pick.astype(bf16)
    own_place = iota((extra, req_total), 0)
    own = iota((extra, req_total), 1) == own_place + pool_idx * req_dev
    pick_ref[slot_total:, :] = one_hot(jnp.logical_and(own, own_place < req_dev))
    gate = gate * pick
    coarse = gate.astype(bf16)
    coarse_ref[...] = coarse
    fine_ref[...] = (gate - coarse.astype(f32)).astype(bf16)
    spread_ref[...] = one_hot(iota(spread_ref.shape, 1) == 2 * iota(spread_ref.shape, 0))
    for copy in fetched:
        copy.wait()


def gain_columns(gain_ref, part, count):
    gains = gain_ref[...].astype(f32)
    rows = iota(gains.shape, 0)
    first = part * (count // LANES)
    return jnp.concatenate(
        [
            jnp.sum(jnp.where(rows == first + i, gains, 0.0), axis=0, keepdims=True)
            for i in range(count // LANES)
        ],
        axis=1,
    )


def prepare_kernel(req_dev, gain_ref, pick_ref, spread_ref, own_sum_ref, *refs):
    received, (gate_ref, up_ref, side_ref, after_ref, all_ref) = refs[:-5], refs[-5:]
    req_total, col_part = own_sum_ref.shape
    after = own_sum_ref[...]
    for part in received:
        after = after + part[...].astype(f32)
    for place in range(all_ref.shape[0]):
        all_ref[place] = after[place * req_dev : (place + 1) * req_dev]
    after_ref[...] = all_ref[lax.axis_index("pool")]
    gains = gain_columns(gain_ref, lax.axis_index("head"), col_part)
    scaled = (after * gains).astype(bf16)
    squares = jnp.sum(after * after, axis=1, keepdims=True)
    coarse = squares.astype(bf16).astype(f32)
    lane = iota((req_total, LANES), 1)
    side = jnp.where(lane == 0, coarse, jnp.where(lane == 1, squares - coarse, 0.0))
    pick = pick_ref[...]
    picked = dot(pick, scaled).astype(bf16)
    side_ref[...] = dot(pick, side.astype(bf16)).astype(bf16)
    spread = dot(picked, spread_ref[...])
    gate_ref[...] = spread.astype(bf16)
    up_ref[...] = pltpu.roll(spread, 1, 1).astype(bf16)


def expert_kernel(
    distance, slots, part, makes_shared, gate_ref, up_ref, side_ref, weight_ref, *refs
):
    refs = list(refs)
    head_devs = lax.axis_size("head")
    if distance == 0:
        near_ref, semaphores = refs[-2:]
        refs = refs[:-2]
        fetched = start_weights(distance, slots, weight_ref, near_ref, semaphores)
        weight_ref = near_ref
        for copy in fetched:
            copy.wait()
    _, depth, _, ffe = weight_ref.shape
    target = lax.axis_index("head") ^ distance
    if makes_shared:
        shared_weight_ref, out_ref, shared_ref = refs
        share = shared_ref.shape[1] // 2
        extra = share * head_devs
        first = gate_ref.shape[0] - extra
        lhs = jnp.concatenate([gate_ref[first:, :], up_ref[first:, :]], axis=0)
        sums = dot(lhs, shared_weight_ref[0].reshape(2 * depth, ffe))
        side = side_ref[first:, :].astype(f32)
        for place in range(head_devs):
            rows = slice(place * share, (place + 1) * share)
            shared_ref[place, :share, :ffe] = sums[:extra][rows]
            shared_ref[place, share:, :ffe] = sums[extra:][rows]
            shared_ref[place, :share, ffe:] = side[rows]
            shared_ref[place, share:, ffe:] = side[rows]
    else:
        shared_ref, out_ref = refs[0], refs[-1]
    each = min(slots, part)
    for i in range(part // each):
        rows = pl.ds(pl.multiple_of(target * part + i * each, TILE), each)
        lhs = jnp.concatenate([gate_ref[rows, :], up_ref[rows, :]], axis=0)
        sums = dot(lhs, weight_ref[i].reshape(2 * depth, ffe))
        out_ref[2 * i * each : 2 * (i + 1) * each, :ffe] = sums.astype(bf16)
        for k in (2 * i, 2 * i + 1):
            out_ref[k * each : (k + 1) * each, ffe:] = side_ref[rows, :]
    out_ref[2 * part :, :] = shared_ref[target].astype(bf16)


def add_kernel(own_ref, received_ref, later_ref, out_ref, sent_ref):
    out_ref[...] = (own_ref[...].astype(f32) + received_ref[...].astype(f32)).astype(bf16)
    sent_ref[...] = later_ref[...]


def hidden_kernel(width, part, each, *refs):
    parts, out_ref = refs[:-1], refs[-1]
    ffe = out_ref.shape[1]
    total = functools.reduce(jnp.add, [ref[...].astype(f32) for ref in parts])
    blocks = [(2 * i * each, i * each, each) for i in range(part // each)]
    for start, row, count in blocks + [(2 * part, part, out_ref.shape[0] - part)]:
        gates, ups = total[start : start + count], total[start + count : start + 2 * count]
        squares = gates[:, ffe : ffe + 1] + gates[:, ffe + 1 : ffe + 2]
        row_scale = lax.rsqrt(squares / width + epsilon)
        gates, ups = gates[:, :ffe] * row_scale, ups[:, :ffe] * row_scale
        out_ref[row : row + count, :] = (gates / (1.0 + jnp.exp(-gates)) * ups).astype(bf16)


def down_rows(distance, slots, hidden_ref, weight_ref):
    part = weight_ref.shape[0] * slots // lax.axis_size("head")
    each = min(slots, part)
    first = (lax.axis_index("head") ^ distance) * part
    return [
        dot(hidden_ref[i * each : (i + 1) * each, :], weight_ref[(first + i * each) // slots])
        for i in range(part // each)
    ]


def down_kernel(distance, slots, hidden_ref, weight_ref, out_ref):
    out_ref[...] = jnp.concatenate(down_rows(distance, slots, hidden_ref, weight_ref), axis=0)


def combine_kernel(distance, slots, coarse_ref, fine_ref, weight_ref, shared_weight_ref, *refs):
    head_devs = lax.axis_size("head")
    hidden_refs, done_refs = refs[:head_devs], refs[head_devs : 2 * head_devs - 1]
    routed_ref, shared_ref, rows_ref = refs[2 * head_devs - 1 :]
    me = lax.axis_index("head")
    part = weight_ref.shape[0] * slots // head_devs
    last = jnp.concatenate(
        down_rows(distance, slots, hidden_refs[distance], weight_ref), axis=0
    )
    done = {j: ref for j, ref in zip([j for j in range(head_devs) if j != distance], done_refs)}
    for j in range(head_devs):
        rows = pl.ds(pl.multiple_of((me ^ j) * part, TILE), part)
        rows_ref[rows, :] = last if j == distance else done[j][...]
    values = rows_ref[...]
    coarse = values.astype(bf16)
    fine = (values - coarse.astype(f32)).astype(bf16)
    def weighted(gates, rows):
        return lax.dot_general(gates, rows, over_rows, preferred_element_type=f32)

    gates = coarse_ref[...]
    routed = weighted(gates, coarse) + (weighted(gates, fine) + weighted(fine_ref[...], coarse))
    pools, req_dev, _ = routed_ref.shape
    for place in range(pools):
        routed_ref[place] = routed[place * req_dev : (place + 1) * req_dev].astype(bf16)
    share = shared_ref.shape[1]
    shared = jnp.concatenate([ref[part:, :].astype(f32) for ref in hidden_refs], axis=0)
    shared = dot(shared.astype(bf16), shared_weight_ref[0])
    for j in range(head_devs):
        shared_ref[me ^ j] = shared[j * share : (j + 1) * share]


def block_kernel(pieces_ref, shared_ref, after_ref, out_ref):
    req_dev = after_ref.shape[0]
    shared = jnp.concatenate([shared_ref[i] for i in range(shared_ref.shape[0])], axis=0)
    total = after_ref[...] + shared[:req_dev]
    for place in range(pieces_ref.shape[0]):
        total = total + pieces_ref[place].astype(f32)
    out_ref[...] = total.astype(bf16)


def join_kernel(bias_ref, *refs):
    for place, ref in enumerate(refs[:-1]):
        refs[-1][place] = ref[0]


def project_kernel(distances, width, gain_ref, weight_ref, *refs):
    me = lax.axis_index("head")
    count = len(distances)
    block_refs, refs = refs[:count], refs[count:]
    if distances[0] == 0:
        total_ref, side_ref = refs
        total, squares = jnp.zeros(total_ref.shape, f32), 0.0
    else:
        own_ref, given_total_ref, given_side_ref, hidden_ref, out_ref = refs
        total, squares = given_total_ref[...], given_side_ref[:, 0:1]
    for distance, ref in zip(distances, block_refs):
        block = ref[...].astype(f32)
        req_dev, col_part = block.shape
        columns = pl.ds(pl.multiple_of((me ^ distance) * col_part, LANES), col_part)
        if distances[0] != 0:
            hidden_ref[:, columns] = ref[...]
        squares = squares + jnp.sum(block * block, axis=1, keepdims=True)
        scaled = (block * gain_columns(gain_ref, me ^ distance, col_part)).astype(bf16)
        total = total + dot(scaled, weight_ref[columns, :])
    if distances[0] == 0:
        total_ref[...] = total
        side_ref[...] = jnp.broadcast_to(squares, side_ref.shape)
    else:
        columns = pl.ds(pl.multiple_of(me * col_part, LANES), col_part)
        hidden_ref[:, columns] = own_ref[...]
        out_ref[...] = (total * lax.rsqrt(squares / width + epsilon)).astype(bf16)


def per_device(
    queries,
    fresh_pair,
    cache_blocks,
    block_table,
    lengths,
    residual,
    w_output,
    norm_gain,
    routes,
    route_gates,
    w_gate_up,
    w_down,
    shared_gate_up,
    shared_down,
    next_gain,
    w_query_key_value,
):
    pools = lax.axis_size("pool")
    head_devs = lax.axis_size("head")
    req_dev, lane_width = queries.shape
    req_total = block_table.shape[0]
    blk_count, _, block_len, _ = cache_blocks.shape
    exp_dev, col_part, _, ffe = w_gate_up.shape
    width = residual.shape[1]
    slots = min(MOST * pools, req_total)
    slot_total = exp_dev * slots
    extra = -(-req_dev // TILE) * TILE
    small = pools <= 8
    distances = list(range(1, head_devs))
    piece_experts = max(1, exp_dev // head_devs)
    fetch_shape = ((piece_experts, col_part, 2, ffe), bf16)
    fetched = list(reversed(range(1, head_devs)))

    queries = queries[None]
    table, counts = block_table.T, lengths[None, :]
    later = [queries, table, counts, cache_blocks, fresh_pair, residual, w_gate_up]
    (early,) = call(
        early_kernel,
        "early",
        [((1,), jnp.int32)],
        later,
        far=range(len(later)),
        megabytes=59,
    )
    (bias,) = call(
        functools.partial(setup_kernel, blk_count, block_len),
        "setup",
        [((req_total, blk_count * block_len), f32)],
        [early, table, counts],
        megabytes=4 + 16 * req_total * blk_count * block_len / 2**20,
    )
    if small:
        order = list(range(0, pools, 2))
        pieces = [queries] + [swap(queries, "pool", d) for d in order[1:]]
        (joined,) = call(
            join_kernel,
            "join_queries",
            [((len(order), req_dev, lane_width), bf16)],
            [bias] + pieces,
            far=[0],
        )
        pieces = [joined, swap(joined, "pool", 1)]
        order = order + [d + 1 for d in order]
    else:
        step = 1
        order, pieces = [0], [queries]
        while step < pools:
            whole = queries if step == 1 else jnp.concatenate(pieces, axis=0)
            pieces.append(swap(whole, "pool", step))
            order += [d ^ step for d in order]
            step *= 2
    (partial,) = call(
        functools.partial(attention_kernel, order),
        "attention",
        [((req_total, lane_width + LANES), bf16)],
        [cache_blocks, bias, fresh_pair, residual] + pieces,
        scratch=[((pools, req_dev, lane_width), f32)],
        megabytes=4 + 32 * req_total * blk_count * block_len / 2**20,
    )
    parts = lax.all_gather(partial, "pool", axis=0)
    sums = call(
        functools.partial(merge_kernel, req_dev),
        "merge_project",
        [((req_total, col_part), f32)] + [((req_total, col_part), bf16)] * (head_devs - 1),
        [parts, w_output],
        scratch=[((req_total, lane_width), bf16)],
        megabytes=5 + 12 * pools * req_total * LANES / 2**20,
    )
    pick, gate_coarse, gate_fine, spread, *weights = call(
        functools.partial(routing_kernel, fetched, slots, req_dev),
        "routing",
        [
            ((slot_total + extra, req_total), bf16),
            ((slot_total, req_total), bf16),
            ((slot_total, req_total), bf16),
            ((col_part, 2 * col_part), bf16),
        ]
        + [fetch_shape] * len(fetched),
        [routes.T, route_gates.T, sums[0], w_gate_up],
        far=[3],
        copies=[len(fetched) * piece_experts * SPLIT],
        megabytes=24,
        moved=2e7,
    )
    weights = dict(zip(fetched, weights))
    received = {d: swap(sums[d], "head", d) for d in reversed(distances)}
    gate_rows, up_rows, side, own_after = call(
        functools.partial(prepare_kernel, req_dev),
        "prepare",
        [
            ((slot_total + extra, 2 * col_part), bf16),
            ((slot_total + extra, 2 * col_part), bf16),
            ((slot_total + extra, LANES), bf16),
            ((req_dev, col_part), f32),
        ],
        [norm_gain.reshape(-1, LANES), pick, spread, sums[0]] + [received[d] for d in distances],
        scratch=[((pools, req_dev, col_part), f32)],
        megabytes=6,
    )

    piece = slot_total // head_devs + extra // head_devs
    part = slot_total // head_devs
    piece_shape = ((2 * piece, ffe + LANES), bf16)
    shared_shape = ((head_devs, 2 * extra // head_devs, ffe + LANES), f32)
    shared_rows = None
    last = head_devs - 1

    def experts(distance, after=()):
        nonlocal shared_rows
        args = [gate_rows, up_rows, side, weights.get(distance, w_gate_up)]
        outs, scratch, copies, far = [piece_shape], [], [], []
        if shared_rows is None:
            args, outs = args + [shared_gate_up], outs + [shared_shape]
        else:
            args = args + [shared_rows] + list(after)
        if distance == 0:
            scratch, copies, far = [fetch_shape], [piece_experts * SPLIT], [3]
        mine, *shared = call(
            functools.partial(expert_kernel, distance, slots, part, len(outs) > 1),
            f"experts_{distance}",
            outs,
            args,
            scratch=scratch,
            copies=copies,
            far=far,
            megabytes=32 if distance == 0 else 10,
        )
        if shared:
            (shared_rows,) = shared
        return mine

    if head_devs == 4:
        near = swap(experts(2), "head", 1)
        own_near = experts(1)
        pair, own_near = call(
            add_kernel,
            "add_pair",
            [piece_shape, piece_shape],
            [experts(3, [own_near]), near, own_near],
        )
        far = swap(pair, "head", 3)
        parts = [experts(0, [pair]), far, swap(own_near, "head", 1)]
    else:
        parts = [swap(experts(d), "head", d) for d in reversed(range(1, head_devs))]
        parts = [experts(0)] + parts
    (hidden,) = call(
        functools.partial(hidden_kernel, width, part, min(slots, part)),
        "hidden",
        [((piece, ffe), bf16)],
        parts,
    )
    hiddens = {0: hidden}
    for d in distances:
        hiddens[d] = swap(hidden, "head", d)
    done = []
    for d in range(last):
        done += call(
            functools.partial(down_kernel, d, slots),
            f"down_{d}",
            [((slot_total // head_devs, col_part), f32)],
            [hiddens[d], w_down],
            megabytes=6,
            )
    routed, shared_out = call(
        functools.partial(combine_kernel, last, slots),
        "combine",
        [((pools, req_dev, col_part), bf16), ((head_devs, extra // head_devs, col_part), f32)],
        [gate_coarse, gate_fine, w_down, shared_down]
        + [hiddens[d] for d in range(head_devs)]
        + done,
        scratch=[((slot_total, col_part), f32)],
        megabytes=6,
    )
    pieces = lax.all_to_all(routed, "pool", 0, 0)
    (block,) = call(
        block_kernel,
        "block",
        [((req_dev, col_part), bf16)],
        [pieces, shared_out, own_after],
        megabytes=4,
    )
    blocks = [block] + [swap(block, "head", d) for d in distances]
    last_args = [next_gain.reshape(-1, LANES), w_query_key_value]
    out_width = w_query_key_value.shape[1]
    total, squares = call(
        functools.partial(project_kernel, [0], width),
        "project_own",
        [((req_dev, out_width), f32), ((req_dev, LANES), f32)],
        last_args + [block],
        megabytes=6,
    )
    next_hidden, next_projection = call(
        functools.partial(project_kernel, distances, width),
        "project",
        [((req_dev, width), bf16), ((req_dev, out_width), bf16)],
        last_args + blocks[1:] + [block, total, squares],
        megabytes=6,
    )
    return (next_hidden, next_projection)


def solution(mesh):
    in_specs = (
        P("pool", "head"),
        P("pool", None, "head"),
        P("pool", None, None, "head"),
        P(),
        P(),
        P("pool", None),
        P("head", None),
        P(),
        P(),
        P(),
        P("pool", "head", None, None),
        P("pool", None, "head"),
        P(None, "head", None, None),
        P(None, None, "head"),
        P(),
        P(None, "head"),
    )
    out_specs = (P("pool", None), P("pool", "head"))
    return jax.shard_map(
        per_device, mesh=mesh, in_specs=in_specs, out_specs=out_specs, check_vma=False
    )
```

```python
import functools
import math

import jax
import jax.numpy as jnp
from jax import lax
from jax.experimental import pallas as pl
from jax.experimental.pallas import tpu as pltpu
from jax.sharding import PartitionSpec as P

HD = 128
LANES = 128
TILE = 16
MOST = 2
SPLIT = 4
HALF = LANES // 2


epsilon = 1e-06
floor_score = -1e30
least_score = -1e29
bf16 = jnp.bfloat16
f32 = jnp.float32
over_rows = (((0,), (0,)), ((), ()))
VMEM = pl.BlockSpec(memory_space=pltpu.VMEM)
SMEM = pl.BlockSpec(memory_space=pltpu.SMEM)
FAR = pl.BlockSpec(memory_space=pltpu.HBM)


def iota(shape, dim):
    return lax.broadcasted_iota(jnp.int32, shape, dim)


def one_hot(mask):
    return mask.astype(f32).astype(bf16)


def dot(left, right):
    return jnp.dot(left, right, preferred_element_type=f32)


def place(shape):
    return SMEM if shape == (1,) else VMEM


def call(kernel, name, outs, args, scratch=(), copies=(), far=(), megabytes=4, moved=1e5):
    semaphores = [pltpu.SemaphoreType.DMA((count,)) for count in copies]
    return pl.pallas_call(
        kernel,
        out_shape=[jax.ShapeDtypeStruct(shape, dtype) for shape, dtype in outs],
        in_specs=[FAR if i in far else place(arg.shape) for i, arg in enumerate(args)],
        out_specs=[place(shape) for shape, _ in outs],
        scratch_shapes=[pltpu.VMEM(shape, dtype) for shape, dtype in scratch] + semaphores,
        compiler_params=pltpu.CompilerParams(vmem_limit_bytes=int(megabytes * 2**20)),
        cost_estimate=pl.CostEstimate(
            flops=1000, bytes_accessed=int(moved), transcendentals=0
        ),
        name=name,
    )(*args)


def swap(value, axis, distance):
    count = lax.axis_size(axis)
    return lax.ppermute(value, axis, [(i, i ^ distance) for i in range(count)])


def start_weights(distance, slots, weight_ref, out_ref, semaphores):
    count, depth = out_ref.shape[:2]
    part = weight_ref.shape[0] * slots // lax.axis_size("head")
    first = (lax.axis_index("head") ^ distance) * part // slots
    rows = depth // SPLIT
    copies = [
        pltpu.make_async_copy(
            weight_ref.at[first + i, pl.ds(k * rows, rows)],
            out_ref.at[i, pl.ds(k * rows, rows)],
            semaphores.at[i * SPLIT + k],
        )
        for i in range(count)
        for k in range(SPLIT)
    ]
    for copy in copies:
        copy.start()
    return copies


def start_all_weights(distances, slots, weight_ref, out_refs, semaphores):
    copies = []
    for place, (distance, out_ref) in enumerate(zip(distances, out_refs)):
        count = out_ref.shape[0] * SPLIT
        own = semaphores.at[pl.ds(place * count, count)]
        copies += start_weights(distance, slots, weight_ref, out_ref, own)
    return copies


def early_kernel(*refs):
    refs[-1][0] = 0


def setup_kernel(blocks, block_len, early_ref, table_ref, length_ref, bias_ref):
    pool_idx = lax.axis_index("pool")
    list_len, req_total = table_ref.shape
    tokens = blocks * block_len
    table = table_ref[...] - pool_idx * blocks
    left = length_ref[...] - iota((list_len, req_total), 0) * block_len
    block_row = iota((LANES, req_total), 0)
    limits = jnp.zeros((LANES, req_total), f32)
    for block in range(blocks):
        found = jnp.sum(jnp.where(table == block, left, 0).astype(f32), axis=0, keepdims=True)
        limits = jnp.where(block_row == block, found, limits)
    limits = jnp.clip(limits, 0.0, float(block_len)).astype(bf16)
    expand = iota((LANES, tokens), 1) // block_len == iota((LANES, tokens), 0)
    limits = lax.dot_general(limits, one_hot(expand), over_rows, preferred_element_type=f32)
    within = lax.rem(iota((1, tokens), 1), block_len).astype(f32)
    bias_ref[...] = jnp.where(within < limits, 0.0, floor_score)


def attention_kernel(
    order,
    cache_ref,
    bias_ref,
    fresh_ref,
    residual_ref,
    *refs,
):
    *query_refs, out_ref, queries_ref = refs
    blocks, _, block_len, _ = cache_ref.shape
    pool_idx = lax.axis_index("pool")
    pools, req_dev, lane_width = queries_ref.shape
    req_total = pools * req_dev
    tokens = blocks * block_len
    scale = math.log2(math.e) / math.sqrt(HD)
    bias = bias_ref[...]
    pieces = [ref[i] for ref in query_refs for i in range(ref.shape[0])]
    for distance, piece in zip(order, pieces):
        queries_ref[pool_idx ^ distance] = piece.astype(f32)
    queries = jnp.concatenate([queries_ref[i] for i in range(pools)], axis=0).astype(bf16)
    own = iota((req_total, req_dev), 0) == iota((req_total, req_dev), 1) + pool_idx * req_dev
    own_bias = jnp.where(own, 0.0, floor_score)
    lane = iota((req_total, LANES), 1)
    side = jnp.zeros((req_total, LANES), f32)
    heads = lane_width // HD
    contract = (((1,), (1,)), ((), ()))
    for head in range(heads):
        columns = slice(head * HD, (head + 1) * HD)
        query = queries[:, columns]
        keys = cache_ref[:, 0, :, columns].reshape(tokens, HD)
        scores = lax.dot_general(query, keys, contract, preferred_element_type=f32) * scale + bias
        new_scores = (
            lax.dot_general(query, fresh_ref[:, 0, columns], contract, preferred_element_type=f32)
            * scale
            + own_bias
        )
        top = jnp.maximum(
            jnp.max(scores, axis=1, keepdims=True), jnp.max(new_scores, axis=1, keepdims=True)
        )
        top = jnp.maximum(top, least_score).astype(bf16).astype(f32)
        weights = jnp.exp2(scores - top)
        new_weights = jnp.exp2(new_scores - top)
        total = jnp.sum(weights, axis=1, keepdims=True) + jnp.sum(
            new_weights, axis=1, keepdims=True
        )
        values = cache_ref[:, 1, :, columns].reshape(tokens, HD)
        mixed = dot(weights.astype(bf16), values) + dot(
            new_weights.astype(bf16), fresh_ref[:, 1, columns]
        )
        inverse = jnp.where(total > 0.0, 1.0 / jnp.where(total > 0.0, total, 1.0), 0.0)
        out_ref[:, columns] = (mixed * inverse).astype(bf16)
        coarse = total.astype(bf16).astype(f32)
        side = jnp.where(lane == head, top, side)
        side = jnp.where(lane == heads + head, coarse, side)
        side = jnp.where(lane == 2 * heads + head, total - coarse, side)
    out_ref[:, lane_width:] = side.astype(bf16)
    start = pl.multiple_of(lax.axis_index("head") * lane_width, LANES)
    residual = residual_ref[:, pl.ds(start, lane_width)]
    for i in range(lane_width // HALF):
        rows = slice(i * req_dev, (i + 1) * req_dev)
        out_ref[rows, lane_width + HALF :] = residual[:, i * HALF : (i + 1) * HALF]


def merge_kernel(req_dev, parts_ref, weight_ref, *refs):
    out_refs, attended_ref = refs[:-1], refs[-1]
    count, req_total, packed = parts_ref.shape
    col_part = out_refs[0].shape[1]
    lane_width = packed - LANES
    heads = lane_width // HD
    me = lax.axis_index("head")
    sides = [parts_ref[i, :, lane_width:].astype(f32) for i in range(count)]
    lane = iota((req_total, LANES), 1)
    tops = [jnp.where(lane < heads, side, 0.0) for side in sides]
    top = functools.reduce(jnp.maximum, tops)

    def shifted(side, by):
        return pltpu.roll(side, LANES - by, 1)

    shares = [
        (shifted(side, heads) + shifted(side, 2 * heads)) * jnp.exp2(part - top)
        for side, part in zip(sides, tops)
    ]
    denominator = functools.reduce(jnp.add, shares)
    inverse = 1.0 / jnp.where(lane < heads, denominator, 1.0)
    spread = iota((2 * LANES, lane_width), 1) // HD == lax.rem(
        iota((2 * LANES, lane_width), 0), LANES
    )
    spread = one_hot(spread)
    mixed = jnp.zeros((req_total, lane_width), f32)
    for i, share in enumerate(shares):
        share = jnp.where(lane < heads, share * inverse, 0.0)
        coarse = share.astype(bf16)
        fine = (share - coarse.astype(f32)).astype(bf16)
        weight = dot(jnp.concatenate([coarse, fine], axis=1), spread)
        mixed = mixed + weight * parts_ref[i, :, :lane_width].astype(f32)
    attended_ref[...] = mixed.astype(bf16)
    for distance, out_ref in enumerate(out_refs):
        start = pl.multiple_of((me ^ distance) * col_part, LANES)
        projected = dot(attended_ref[...], weight_ref[:, pl.ds(start, col_part)])
        out_ref[...] = projected.astype(out_ref.dtype)
    for i, side in enumerate(sides):
        rows = slice(i * req_dev, (i + 1) * req_dev)
        pieces = [
            side[k * req_dev : (k + 1) * req_dev, HALF:] for k in range(lane_width // HALF)
        ]
        out_refs[0][rows, :] = out_refs[0][rows, :] + jnp.concatenate(pieces, axis=1)


def routing_kernel(
    distances,
    slots,
    req_dev,
    routes_ref,
    gates_ref,
    after_ref,
    far_weight_ref,
    pick_ref,
    coarse_ref,
    fine_ref,
    spread_ref,
    *refs,
):
    weight_refs, semaphores = refs[:-1], refs[-1]
    fetched = start_all_weights(distances, slots, far_weight_ref, weight_refs, semaphores)
    top_k, req_total = routes_ref.shape
    slot_total = coarse_ref.shape[0]
    extra = pick_ref.shape[0] - slot_total
    pool_idx = lax.axis_index("pool")
    expert = iota((slot_total, req_total), 0) // slots + pool_idx * (slot_total // slots)
    rank = lax.rem(iota((slot_total, req_total), 0), slots).astype(f32)
    chosen = jnp.zeros((slot_total, req_total), f32)
    gate = jnp.zeros((slot_total, req_total), f32)
    for k in range(top_k):
        match = routes_ref[k : k + 1, :] == expert
        chosen = jnp.where(match, 1.0, chosen)
        gate = jnp.where(match, gates_ref[k : k + 1, :], gate)
    earlier = iota((req_total, req_total), 0) < iota((req_total, req_total), 1)
    place = dot(chosen.astype(bf16), one_hot(earlier))
    pick = jnp.where(place == rank, chosen, 0.0)
    pick_ref[:slot_total, :] = pick.astype(bf16)
    own_place = iota((extra, req_total), 0)
    own = iota((extra, req_total), 1) == own_place + pool_idx * req_dev
    pick_ref[slot_total:, :] = one_hot(jnp.logical_and(own, own_place < req_dev))
    gate = gate * pick
    coarse = gate.astype(bf16)
    coarse_ref[...] = coarse
    fine_ref[...] = (gate - coarse.astype(f32)).astype(bf16)
    spread_ref[...] = one_hot(iota(spread_ref.shape, 1) == 2 * iota(spread_ref.shape, 0))
    for copy in fetched:
        copy.wait()


def gain_columns(gain_ref, part, count):
    gains = gain_ref[...].astype(f32)
    rows = iota(gains.shape, 0)
    first = part * (count // LANES)
    return jnp.concatenate(
        [
            jnp.sum(jnp.where(rows == first + i, gains, 0.0), axis=0, keepdims=True)
            for i in range(count // LANES)
        ],
        axis=1,
    )


def prepare_kernel(req_dev, gain_ref, pick_ref, spread_ref, own_sum_ref, *refs):
    received, (gate_ref, up_ref, side_ref, after_ref, all_ref) = refs[:-5], refs[-5:]
    req_total, col_part = own_sum_ref.shape
    after = own_sum_ref[...]
    for part in received:
        after = after + part[...].astype(f32)
    for place in range(all_ref.shape[0]):
        all_ref[place] = after[place * req_dev : (place + 1) * req_dev]
    after_ref[...] = all_ref[lax.axis_index("pool")]
    gains = gain_columns(gain_ref, lax.axis_index("head"), col_part)
    scaled = (after * gains).astype(bf16)
    squares = jnp.sum(after * after, axis=1, keepdims=True)
    coarse = squares.astype(bf16).astype(f32)
    lane = iota((req_total, LANES), 1)
    side = jnp.where(lane == 0, coarse, jnp.where(lane == 1, squares - coarse, 0.0))
    pick = pick_ref[...]
    picked = dot(pick, scaled).astype(bf16)
    side_ref[...] = dot(pick, side.astype(bf16)).astype(bf16)
    spread = dot(picked, spread_ref[...])
    gate_ref[...] = spread.astype(bf16)
    up_ref[...] = pltpu.roll(spread, 1, 1).astype(bf16)


def expert_kernel(
    distance, slots, part, makes_shared, gate_ref, up_ref, side_ref, weight_ref, *refs
):
    refs = list(refs)
    head_devs = lax.axis_size("head")
    if distance < 2:
        near_ref, semaphores = refs[-2:]
        refs = refs[:-2]
        fetched = start_weights(distance, slots, weight_ref, near_ref, semaphores)
        weight_ref = near_ref
        for copy in fetched:
            copy.wait()
    _, depth, _, ffe = weight_ref.shape
    target = lax.axis_index("head") ^ distance
    if makes_shared:
        shared_weight_ref, out_ref, shared_ref = refs
        share = shared_ref.shape[1] // 2
        extra = share * head_devs
        first = gate_ref.shape[0] - extra
        lhs = jnp.concatenate([gate_ref[first:, :], up_ref[first:, :]], axis=0)
        sums = dot(lhs, shared_weight_ref[0].reshape(2 * depth, ffe))
        side = side_ref[first:, :].astype(f32)
        for place in range(head_devs):
            rows = slice(place * share, (place + 1) * share)
            shared_ref[place, :share, :ffe] = sums[:extra][rows]
            shared_ref[place, share:, :ffe] = sums[extra:][rows]
            shared_ref[place, :share, ffe:] = side[rows]
            shared_ref[place, share:, ffe:] = side[rows]
    else:
        shared_ref, out_ref = refs[0], refs[-1]
    each = min(slots, part)
    for i in range(part // each):
        rows = pl.ds(pl.multiple_of(target * part + i * each, TILE), each)
        lhs = jnp.concatenate([gate_ref[rows, :], up_ref[rows, :]], axis=0)
        sums = dot(lhs, weight_ref[i].reshape(2 * depth, ffe))
        out_ref[2 * i * each : 2 * (i + 1) * each, :ffe] = sums.astype(bf16)
        for k in (2 * i, 2 * i + 1):
            out_ref[k * each : (k + 1) * each, ffe:] = side_ref[rows, :]
    out_ref[2 * part :, :] = shared_ref[target].astype(bf16)


def add_kernel(own_ref, received_ref, later_ref, out_ref, sent_ref):
    out_ref[...] = (own_ref[...].astype(f32) + received_ref[...].astype(f32)).astype(bf16)
    sent_ref[...] = later_ref[...]


def hidden_kernel(width, part, each, *refs):
    parts, out_ref = refs[:-1], refs[-1]
    ffe = out_ref.shape[1]
    total = functools.reduce(jnp.add, [ref[...].astype(f32) for ref in parts])
    blocks = [(2 * i * each, i * each, each) for i in range(part // each)]
    for start, row, count in blocks + [(2 * part, part, out_ref.shape[0] - part)]:
        gates, ups = total[start : start + count], total[start + count : start + 2 * count]
        squares = gates[:, ffe : ffe + 1] + gates[:, ffe + 1 : ffe + 2]
        row_scale = lax.rsqrt(squares / width + epsilon)
        gates, ups = gates[:, :ffe] * row_scale, ups[:, :ffe] * row_scale
        out_ref[row : row + count, :] = (gates / (1.0 + jnp.exp(-gates)) * ups).astype(bf16)


def down_rows(distance, slots, hidden_ref, weight_ref):
    part = weight_ref.shape[0] * slots // lax.axis_size("head")
    each = min(slots, part)
    first = (lax.axis_index("head") ^ distance) * part
    return [
        dot(hidden_ref[i * each : (i + 1) * each, :], weight_ref[(first + i * each) // slots])
        for i in range(part // each)
    ]


def down_kernel(distance, slots, hidden_ref, weight_ref, out_ref):
    out_ref[...] = jnp.concatenate(down_rows(distance, slots, hidden_ref, weight_ref), axis=0)


def combine_kernel(distance, slots, coarse_ref, fine_ref, weight_ref, shared_weight_ref, *refs):
    head_devs = lax.axis_size("head")
    hidden_refs, done_refs = refs[:head_devs], refs[head_devs : 2 * head_devs - 1]
    routed_ref, shared_ref, rows_ref = refs[2 * head_devs - 1 :]
    me = lax.axis_index("head")
    part = weight_ref.shape[0] * slots // head_devs
    last = jnp.concatenate(
        down_rows(distance, slots, hidden_refs[distance], weight_ref), axis=0
    )
    done = {j: ref for j, ref in zip([j for j in range(head_devs) if j != distance], done_refs)}
    for j in range(head_devs):
        rows = pl.ds(pl.multiple_of((me ^ j) * part, TILE), part)
        rows_ref[rows, :] = last if j == distance else done[j][...]
    values = rows_ref[...]
    coarse = values.astype(bf16)
    fine = (values - coarse.astype(f32)).astype(bf16)
    def weighted(gates, rows):
        return lax.dot_general(gates, rows, over_rows, preferred_element_type=f32)

    gates = coarse_ref[...]
    routed = weighted(gates, coarse) + (weighted(gates, fine) + weighted(fine_ref[...], coarse))
    pools, req_dev, _ = routed_ref.shape
    for place in range(pools):
        routed_ref[place] = routed[place * req_dev : (place + 1) * req_dev].astype(bf16)
    share = shared_ref.shape[1]
    shared = jnp.concatenate([ref[part:, :].astype(f32) for ref in hidden_refs], axis=0)
    shared = dot(shared.astype(bf16), shared_weight_ref[0])
    for j in range(head_devs):
        shared_ref[me ^ j] = shared[j * share : (j + 1) * share]


def block_kernel(pieces_ref, shared_ref, after_ref, out_ref):
    req_dev = after_ref.shape[0]
    shared = jnp.concatenate([shared_ref[i] for i in range(shared_ref.shape[0])], axis=0)
    total = after_ref[...] + shared[:req_dev]
    for place in range(pieces_ref.shape[0]):
        total = total + pieces_ref[place].astype(f32)
    out_ref[...] = total.astype(bf16)


def join_kernel(bias_ref, *refs):
    for place, ref in enumerate(refs[:-1]):
        refs[-1][place] = ref[0]


def project_kernel(distances, width, begins, ends, gain_ref, weight_ref, *refs):
    me = lax.axis_index("head")
    count = len(distances)
    block_refs, refs = refs[:count], refs[count:]
    total, squares = 0.0, 0.0
    if not begins:
        total, squares = refs[0][...], refs[1][:, 0:1]
        refs = refs[2:]
    for distance, ref in zip(distances, block_refs):
        block = ref[...].astype(f32)
        col_part = block.shape[1]
        rows = pl.ds(pl.multiple_of((me ^ distance) * col_part, LANES), col_part)
        squares = squares + jnp.sum(block * block, axis=1, keepdims=True)
        scaled = (block * gain_columns(gain_ref, me ^ distance, col_part)).astype(bf16)
        total = total + dot(scaled, weight_ref[rows, :])
    if not ends:
        refs[0][...] = total
        refs[1][...] = jnp.broadcast_to(squares, refs[1].shape)
        return
    *every_refs, hidden_ref, out_ref = refs
    out_ref[...] = (total * lax.rsqrt(squares / width + epsilon)).astype(bf16)
    for distance, ref in enumerate(every_refs):
        columns = pl.ds(pl.multiple_of((me ^ distance) * ref.shape[1], LANES), ref.shape[1])
        hidden_ref[:, columns] = ref[...]


def per_device(
    queries,
    fresh_pair,
    cache_blocks,
    block_table,
    lengths,
    residual,
    w_output,
    norm_gain,
    routes,
    route_gates,
    w_gate_up,
    w_down,
    shared_gate_up,
    shared_down,
    next_gain,
    w_query_key_value,
):
    pools = lax.axis_size("pool")
    head_devs = lax.axis_size("head")
    req_dev, lane_width = queries.shape
    req_total = block_table.shape[0]
    blk_count, _, block_len, _ = cache_blocks.shape
    exp_dev, col_part, _, ffe = w_gate_up.shape
    width = residual.shape[1]
    slots = min(MOST * pools, req_total)
    slot_total = exp_dev * slots
    extra = -(-req_dev // TILE) * TILE
    small = pools <= 8
    distances = list(range(1, head_devs))
    piece_experts = max(1, exp_dev // head_devs)
    fetch_shape = ((piece_experts, col_part, 2, ffe), bf16)
    fetched = list(reversed(range(2, head_devs)))

    queries = queries[None]
    table, counts = block_table.T, lengths[None, :]
    later = [queries, table, counts, cache_blocks, fresh_pair, residual, w_gate_up]
    (early,) = call(
        early_kernel,
        "early",
        [((1,), jnp.int32)],
        later,
        far=range(len(later)),
        megabytes=59,
    )
    (bias,) = call(
        functools.partial(setup_kernel, blk_count, block_len),
        "setup",
        [((req_total, blk_count * block_len), f32)],
        [early, table, counts],
        megabytes=4 + 16 * req_total * blk_count * block_len / 2**20,
    )
    if small:
        order = list(range(0, pools, 2))
        pieces = [queries] + [swap(queries, "pool", d) for d in order[1:]]
        (joined,) = call(
            join_kernel,
            "join_queries",
            [((len(order), req_dev, lane_width), bf16)],
            [bias] + pieces,
            far=[0],
        )
        pieces = [joined, swap(joined, "pool", 1)]
        order = order + [d + 1 for d in order]
    else:
        step = 1
        order, pieces = [0], [queries]
        while step < pools:
            whole = queries if step == 1 else jnp.concatenate(pieces, axis=0)
            pieces.append(swap(whole, "pool", step))
            order += [d ^ step for d in order]
            step *= 2
    (partial,) = call(
        functools.partial(attention_kernel, order),
        "attention",
        [((req_total, lane_width + LANES), bf16)],
        [cache_blocks, bias, fresh_pair, residual] + pieces,
        scratch=[((pools, req_dev, lane_width), f32)],
        megabytes=4 + 32 * req_total * blk_count * block_len / 2**20,
    )
    parts = lax.all_gather(partial, "pool", axis=0)
    sums = call(
        functools.partial(merge_kernel, req_dev),
        "merge_project",
        [((req_total, col_part), f32)] + [((req_total, col_part), bf16)] * (head_devs - 1),
        [parts, w_output],
        scratch=[((req_total, lane_width), bf16)],
        megabytes=5 + 12 * pools * req_total * LANES / 2**20,
    )
    pick, gate_coarse, gate_fine, spread, *weights = call(
        functools.partial(routing_kernel, fetched, slots, req_dev),
        "routing",
        [
            ((slot_total + extra, req_total), bf16),
            ((slot_total, req_total), bf16),
            ((slot_total, req_total), bf16),
            ((col_part, 2 * col_part), bf16),
        ]
        + [fetch_shape] * len(fetched),
        [routes.T, route_gates.T, sums[0], w_gate_up],
        far=[3],
        copies=[len(fetched) * piece_experts * SPLIT],
        megabytes=24,
        moved=2e7,
    )
    weights = dict(zip(fetched, weights))
    received = {d: swap(sums[d], "head", d) for d in reversed(distances)}
    gate_rows, up_rows, side, own_after = call(
        functools.partial(prepare_kernel, req_dev),
        "prepare",
        [
            ((slot_total + extra, 2 * col_part), bf16),
            ((slot_total + extra, 2 * col_part), bf16),
            ((slot_total + extra, LANES), bf16),
            ((req_dev, col_part), f32),
        ],
        [norm_gain.reshape(-1, LANES), pick, spread, sums[0]] + [received[d] for d in distances],
        scratch=[((pools, req_dev, col_part), f32)],
        megabytes=6,
    )

    piece = slot_total // head_devs + extra // head_devs
    part = slot_total // head_devs
    piece_shape = ((2 * piece, ffe + LANES), bf16)
    shared_shape = ((head_devs, 2 * extra // head_devs, ffe + LANES), f32)
    shared_rows = None
    last = head_devs - 1

    def experts(distance, after=()):
        nonlocal shared_rows
        args = [gate_rows, up_rows, side, weights.get(distance, w_gate_up)]
        outs, scratch, copies, far = [piece_shape], [], [], []
        if shared_rows is None:
            args, outs = args + [shared_gate_up], outs + [shared_shape]
        else:
            args = args + [shared_rows] + list(after)
        if distance < 2:
            scratch, copies, far = [fetch_shape], [piece_experts * SPLIT], [3]
        mine, *shared = call(
            functools.partial(expert_kernel, distance, slots, part, len(outs) > 1),
            f"experts_{distance}",
            outs,
            args,
            scratch=scratch,
            copies=copies,
            far=far,
            megabytes=32 if distance < 2 else 10,
        )
        if shared:
            (shared_rows,) = shared
        return mine

    if head_devs == 4:
        near = swap(experts(2), "head", 1)
        own_near = experts(1)
        pair, own_near = call(
            add_kernel,
            "add_pair",
            [piece_shape, piece_shape],
            [experts(3, [own_near]), near, own_near],
        )
        far = swap(pair, "head", 3)
        parts = [experts(0, [pair]), far, swap(own_near, "head", 1)]
    else:
        parts = [swap(experts(d), "head", d) for d in reversed(range(1, head_devs))]
        parts = [experts(0)] + parts
    (hidden,) = call(
        functools.partial(hidden_kernel, width, part, min(slots, part)),
        "hidden",
        [((piece, ffe), bf16)],
        parts,
    )
    hiddens = {0: hidden}
    for d in distances:
        hiddens[d] = swap(hidden, "head", d)
    done = []
    for d in range(last):
        done += call(
            functools.partial(down_kernel, d, slots),
            f"down_{d}",
            [((slot_total // head_devs, col_part), f32)],
            [hiddens[d], w_down],
            megabytes=6,
            )
    routed, shared_out = call(
        functools.partial(combine_kernel, last, slots),
        "combine",
        [((pools, req_dev, col_part), bf16), ((head_devs, extra // head_devs, col_part), f32)],
        [gate_coarse, gate_fine, w_down, shared_down]
        + [hiddens[d] for d in range(head_devs)]
        + done,
        scratch=[((slot_total, col_part), f32)],
        megabytes=6,
    )
    pieces = lax.all_to_all(routed, "pool", 0, 0)
    (block,) = call(
        block_kernel,
        "block",
        [((req_dev, col_part), bf16)],
        [pieces, shared_out, own_after],
        megabytes=4,
    )
    blocks = [block] + [swap(block, "head", d) for d in distances]
    last_args = [next_gain.reshape(-1, LANES), w_query_key_value]
    out_width = w_query_key_value.shape[1]
    running = []
    for which in ([0], distances[2:]):
        running = call(
            functools.partial(project_kernel, which, width, not running, False),
            f"project_{which[0]}",
            [((req_dev, out_width), f32), ((req_dev, LANES), f32)],
            last_args + [blocks[d] for d in which] + list(running),
            megabytes=6,
        )
    next_hidden, next_projection = call(
        functools.partial(project_kernel, distances[:2], width, False, True),
        "project",
        [((req_dev, width), bf16), ((req_dev, out_width), bf16)],
        last_args + [blocks[d] for d in distances[:2]] + list(running) + blocks,
        megabytes=6,
    )
    return (next_hidden, next_projection)


def solution(mesh):
    in_specs = (
        P("pool", "head"),
        P("pool", None, "head"),
        P("pool", None, None, "head"),
        P(),
        P(),
        P("pool", None),
        P("head", None),
        P(),
        P(),
        P(),
        P("pool", "head", None, None),
        P("pool", None, "head"),
        P(None, "head", None, None),
        P(None, None, "head"),
        P(),
        P(None, "head"),
    )
    out_specs = (P("pool", None), P("pool", "head"))
    return jax.shard_map(
        per_device, mesh=mesh, in_specs=in_specs, out_specs=out_specs, check_vma=False
    )
```

```python
import functools
import math

import jax
import jax.numpy as jnp
from jax import lax
from jax.experimental import pallas as pl
from jax.experimental.pallas import tpu as pltpu
from jax.sharding import PartitionSpec as P

HD = 128
LANES = 128
TILE = 16
MOST = 2
SPLIT = 4
HALF = LANES // 2


epsilon = 1e-06
floor_score = -1e30
least_score = -1e29
bf16 = jnp.bfloat16
f32 = jnp.float32
over_rows = (((0,), (0,)), ((), ()))
VMEM = pl.BlockSpec(memory_space=pltpu.VMEM)
SMEM = pl.BlockSpec(memory_space=pltpu.SMEM)
FAR = pl.BlockSpec(memory_space=pltpu.HBM)


def iota(shape, dim):
    return lax.broadcasted_iota(jnp.int32, shape, dim)


def one_hot(mask):
    return mask.astype(f32).astype(bf16)


def dot(left, right):
    return jnp.dot(left, right, preferred_element_type=f32)


def place(shape):
    return SMEM if shape == (1,) else VMEM


def call(kernel, name, outs, args, scratch=(), copies=(), far=(), megabytes=4, moved=1e5):
    semaphores = [pltpu.SemaphoreType.DMA((count,)) for count in copies]
    return pl.pallas_call(
        kernel,
        out_shape=[jax.ShapeDtypeStruct(shape, dtype) for shape, dtype in outs],
        in_specs=[FAR if i in far else place(arg.shape) for i, arg in enumerate(args)],
        out_specs=[place(shape) for shape, _ in outs],
        scratch_shapes=[pltpu.VMEM(shape, dtype) for shape, dtype in scratch] + semaphores,
        compiler_params=pltpu.CompilerParams(vmem_limit_bytes=int(megabytes * 2**20)),
        cost_estimate=pl.CostEstimate(
            flops=1000, bytes_accessed=int(moved), transcendentals=0
        ),
        name=name,
    )(*args)


def swap(value, axis, distance):
    count = lax.axis_size(axis)
    return lax.ppermute(value, axis, [(i, i ^ distance) for i in range(count)])


def start_weights(distance, slots, weight_ref, out_ref, semaphores):
    count, depth = out_ref.shape[:2]
    part = weight_ref.shape[0] * slots // lax.axis_size("head")
    first = (lax.axis_index("head") ^ distance) * part // slots
    rows = depth // SPLIT
    copies = [
        pltpu.make_async_copy(
            weight_ref.at[first + i, pl.ds(k * rows, rows)],
            out_ref.at[i, pl.ds(k * rows, rows)],
            semaphores.at[i * SPLIT + k],
        )
        for i in range(count)
        for k in range(SPLIT)
    ]
    for copy in copies:
        copy.start()
    return copies


def start_all_weights(distances, slots, weight_ref, out_refs, semaphores):
    copies = []
    for place, (distance, out_ref) in enumerate(zip(distances, out_refs)):
        count = out_ref.shape[0] * SPLIT
        own = semaphores.at[pl.ds(place * count, count)]
        copies += start_weights(distance, slots, weight_ref, out_ref, own)
    return copies


def early_kernel(*refs):
    refs[-1][0] = 0


def setup_kernel(blocks, block_len, early_ref, table_ref, length_ref, bias_ref):
    pool_idx = lax.axis_index("pool")
    list_len, req_total = table_ref.shape
    tokens = blocks * block_len
    table = table_ref[...] - pool_idx * blocks
    left = length_ref[...] - iota((list_len, req_total), 0) * block_len
    block_row = iota((LANES, req_total), 0)
    limits = jnp.zeros((LANES, req_total), f32)
    for block in range(blocks):
        found = jnp.sum(jnp.where(table == block, left, 0).astype(f32), axis=0, keepdims=True)
        limits = jnp.where(block_row == block, found, limits)
    limits = jnp.clip(limits, 0.0, float(block_len)).astype(bf16)
    expand = iota((LANES, tokens), 1) // block_len == iota((LANES, tokens), 0)
    limits = lax.dot_general(limits, one_hot(expand), over_rows, preferred_element_type=f32)
    within = lax.rem(iota((1, tokens), 1), block_len).astype(f32)
    bias_ref[...] = jnp.where(within < limits, 0.0, floor_score)


def attention_kernel(
    order,
    cache_ref,
    bias_ref,
    fresh_ref,
    residual_ref,
    *refs,
):
    *query_refs, out_ref, queries_ref = refs
    blocks, _, block_len, _ = cache_ref.shape
    pool_idx = lax.axis_index("pool")
    pools, req_dev, lane_width = queries_ref.shape
    req_total = pools * req_dev
    tokens = blocks * block_len
    scale = math.log2(math.e) / math.sqrt(HD)
    bias = bias_ref[...]
    pieces = [ref[i] for ref in query_refs for i in range(ref.shape[0])]
    for distance, piece in zip(order, pieces):
        queries_ref[pool_idx ^ distance] = piece.astype(f32)
    queries = jnp.concatenate([queries_ref[i] for i in range(pools)], axis=0).astype(bf16)
    own = iota((req_total, req_dev), 0) == iota((req_total, req_dev), 1) + pool_idx * req_dev
    own_bias = jnp.where(own, 0.0, floor_score)
    lane = iota((req_total, LANES), 1)
    side = jnp.zeros((req_total, LANES), f32)
    heads = lane_width // HD
    contract = (((1,), (1,)), ((), ()))
    for head in range(heads):
        columns = slice(head * HD, (head + 1) * HD)
        query = queries[:, columns]
        keys = cache_ref[:, 0, :, columns].reshape(tokens, HD)
        scores = lax.dot_general(query, keys, contract, preferred_element_type=f32) * scale + bias
        new_scores = (
            lax.dot_general(query, fresh_ref[:, 0, columns], contract, preferred_element_type=f32)
            * scale
            + own_bias
        )
        top = jnp.maximum(
            jnp.max(scores, axis=1, keepdims=True), jnp.max(new_scores, axis=1, keepdims=True)
        )
        top = jnp.maximum(top, least_score).astype(bf16).astype(f32)
        weights = jnp.exp2(scores - top)
        new_weights = jnp.exp2(new_scores - top)
        total = jnp.sum(weights, axis=1, keepdims=True) + jnp.sum(
            new_weights, axis=1, keepdims=True
        )
        values = cache_ref[:, 1, :, columns].reshape(tokens, HD)
        mixed = dot(weights.astype(bf16), values) + dot(
            new_weights.astype(bf16), fresh_ref[:, 1, columns]
        )
        inverse = jnp.where(total > 0.0, 1.0 / jnp.where(total > 0.0, total, 1.0), 0.0)
        out_ref[:, columns] = (mixed * inverse).astype(bf16)
        coarse = total.astype(bf16).astype(f32)
        side = jnp.where(lane == head, top, side)
        side = jnp.where(lane == heads + head, coarse, side)
        side = jnp.where(lane == 2 * heads + head, total - coarse, side)
    out_ref[:, lane_width:] = side.astype(bf16)
    start = pl.multiple_of(lax.axis_index("head") * lane_width, LANES)
    residual = residual_ref[:, pl.ds(start, lane_width)]
    for i in range(lane_width // HALF):
        rows = slice(i * req_dev, (i + 1) * req_dev)
        out_ref[rows, lane_width + HALF :] = residual[:, i * HALF : (i + 1) * HALF]


def merge_kernel(req_dev, parts_ref, weight_ref, *refs):
    out_refs, attended_ref = refs[:-1], refs[-1]
    count, req_total, packed = parts_ref.shape
    col_part = out_refs[0].shape[1]
    lane_width = packed - LANES
    heads = lane_width // HD
    me = lax.axis_index("head")
    sides = [parts_ref[i, :, lane_width:].astype(f32) for i in range(count)]
    lane = iota((req_total, LANES), 1)
    tops = [jnp.where(lane < heads, side, 0.0) for side in sides]
    top = functools.reduce(jnp.maximum, tops)

    def shifted(side, by):
        return pltpu.roll(side, LANES - by, 1)

    shares = [
        (shifted(side, heads) + shifted(side, 2 * heads)) * jnp.exp2(part - top)
        for side, part in zip(sides, tops)
    ]
    denominator = functools.reduce(jnp.add, shares)
    inverse = 1.0 / jnp.where(lane < heads, denominator, 1.0)
    spread = iota((2 * LANES, lane_width), 1) // HD == lax.rem(
        iota((2 * LANES, lane_width), 0), LANES
    )
    spread = one_hot(spread)
    mixed = jnp.zeros((req_total, lane_width), f32)
    for i, share in enumerate(shares):
        share = jnp.where(lane < heads, share * inverse, 0.0)
        coarse = share.astype(bf16)
        fine = (share - coarse.astype(f32)).astype(bf16)
        weight = dot(jnp.concatenate([coarse, fine], axis=1), spread)
        mixed = mixed + weight * parts_ref[i, :, :lane_width].astype(f32)
    attended_ref[...] = mixed.astype(bf16)
    for distance, out_ref in enumerate(out_refs):
        start = pl.multiple_of((me ^ distance) * col_part, LANES)
        projected = dot(attended_ref[...], weight_ref[:, pl.ds(start, col_part)])
        out_ref[...] = projected.astype(out_ref.dtype)
    for i, side in enumerate(sides):
        rows = slice(i * req_dev, (i + 1) * req_dev)
        pieces = [
            side[k * req_dev : (k + 1) * req_dev, HALF:] for k in range(lane_width // HALF)
        ]
        out_refs[0][rows, :] = out_refs[0][rows, :] + jnp.concatenate(pieces, axis=1)


def routing_kernel(
    distances,
    slots,
    req_dev,
    routes_ref,
    gates_ref,
    after_ref,
    far_weight_ref,
    pick_ref,
    coarse_ref,
    fine_ref,
    spread_ref,
    *refs,
):
    weight_refs, semaphores = refs[:-1], refs[-1]
    fetched = start_all_weights(distances, slots, far_weight_ref, weight_refs, semaphores)
    top_k, req_total = routes_ref.shape
    slot_total = coarse_ref.shape[0]
    extra = pick_ref.shape[0] - slot_total
    pool_idx = lax.axis_index("pool")
    expert = iota((slot_total, req_total), 0) // slots + pool_idx * (slot_total // slots)
    rank = lax.rem(iota((slot_total, req_total), 0), slots).astype(f32)
    chosen = jnp.zeros((slot_total, req_total), f32)
    gate = jnp.zeros((slot_total, req_total), f32)
    for k in range(top_k):
        match = routes_ref[k : k + 1, :] == expert
        chosen = jnp.where(match, 1.0, chosen)
        gate = jnp.where(match, gates_ref[k : k + 1, :], gate)
    earlier = iota((req_total, req_total), 0) < iota((req_total, req_total), 1)
    place = dot(chosen.astype(bf16), one_hot(earlier))
    pick = jnp.where(place == rank, chosen, 0.0)
    pick_ref[:slot_total, :] = pick.astype(bf16)
    own_place = iota((extra, req_total), 0)
    own = iota((extra, req_total), 1) == own_place + pool_idx * req_dev
    pick_ref[slot_total:, :] = one_hot(jnp.logical_and(own, own_place < req_dev))
    gate = gate * pick
    coarse = gate.astype(bf16)
    coarse_ref[...] = coarse
    fine_ref[...] = (gate - coarse.astype(f32)).astype(bf16)
    spread_ref[...] = one_hot(iota(spread_ref.shape, 1) == 2 * iota(spread_ref.shape, 0))
    for copy in fetched:
        copy.wait()


def gain_columns(gain_ref, part, count):
    gains = gain_ref[...].astype(f32)
    rows = iota(gains.shape, 0)
    first = part * (count // LANES)
    return jnp.concatenate(
        [
            jnp.sum(jnp.where(rows == first + i, gains, 0.0), axis=0, keepdims=True)
            for i in range(count // LANES)
        ],
        axis=1,
    )


def prepare_kernel(req_dev, part, share, gain_ref, pick_ref, spread_ref, own_sum_ref, *refs):
    received, (gate_ref, up_ref, side_ref, after_ref, all_ref) = refs[:-5], refs[-5:]
    req_total, col_part = own_sum_ref.shape
    after = own_sum_ref[...]
    for ref in received:
        after = after + ref[...].astype(f32)
    for place in range(all_ref.shape[0]):
        all_ref[place] = after[place * req_dev : (place + 1) * req_dev]
    after_ref[...] = all_ref[lax.axis_index("pool")]
    gains = gain_columns(gain_ref, lax.axis_index("head"), col_part)
    scaled = (after * gains).astype(bf16)
    squares = jnp.sum(after * after, axis=1, keepdims=True)
    coarse = squares.astype(bf16).astype(f32)
    lane = iota((req_total, LANES), 1)
    side = jnp.where(lane == 0, coarse, jnp.where(lane == 1, squares - coarse, 0.0))
    pick = pick_ref[...]
    picked = dot(pick, scaled).astype(bf16)
    same = iota((req_total, req_total), 0) == iota((req_total, req_total), 1)
    turned = lax.dot_general(
        side.astype(bf16), one_hot(same), over_rows, preferred_element_type=f32
    )[:8].astype(bf16)
    contract = (((1,), (1,)), ((), ()))
    lined = lax.dot_general(turned, pick, contract, preferred_element_type=f32)
    targets = side_ref.shape[0]
    for target in range(targets):
        first = targets * part + target * share
        side_ref[target] = jnp.zeros(side_ref.shape[1:], f32)
        side_ref[target, :, :part] = lined[:, target * part : (target + 1) * part]
        side_ref[target, :, part : part + share] = lined[:, first : first + share]
    spread = dot(picked, spread_ref[...])
    gate_ref[...] = spread.astype(bf16)
    up_ref[...] = pltpu.roll(spread, 1, 1).astype(bf16)


def expert_kernel(
    distance, slots, part, makes_shared, gate_ref, up_ref, side_ref, weight_ref, *refs
):
    refs = list(refs)
    head_devs = lax.axis_size("head")
    if distance < 2:
        near_ref, semaphores = refs[-2:]
        refs = refs[:-2]
        fetched = start_weights(distance, slots, weight_ref, near_ref, semaphores)
        weight_ref = near_ref
        for copy in fetched:
            copy.wait()
    _, depth, _, ffe = weight_ref.shape
    target = lax.axis_index("head") ^ distance
    if makes_shared:
        shared_weight_ref, out_ref, shared_ref = refs
        share = shared_ref.shape[1] // 2
        extra = gate_ref.shape[0] - part * head_devs
        first = part * head_devs
        lhs = jnp.concatenate([gate_ref[first:, :], up_ref[first:, :]], axis=0)
        sums = dot(lhs, shared_weight_ref[0].reshape(2 * depth, ffe))
        for place in range(head_devs):
            rows = slice(place * share, (place + 1) * share)
            shared_ref[place, :share, :] = sums[:extra][rows]
            shared_ref[place, share:, :] = sums[extra:][rows]
    else:
        shared_ref, out_ref = refs[0], refs[-1]
    each = min(slots, part)
    for i in range(part // each):
        rows = pl.ds(pl.multiple_of(target * part + i * each, TILE), each)
        lhs = jnp.concatenate([gate_ref[rows, :], up_ref[rows, :]], axis=0)
        sums = dot(lhs, weight_ref[i].reshape(2 * depth, ffe))
        out_ref[2 * i * each : 2 * (i + 1) * each, :] = sums.astype(bf16)
    side = side_ref[target][:2]
    side = jnp.concatenate([side, jnp.zeros((2, ffe - LANES), f32)], axis=1)
    last = jnp.concatenate([shared_ref[target], side], axis=0)
    out_ref[2 * part :, :] = last.astype(bf16)


def add_kernel(own_ref, received_ref, later_ref, out_ref, sent_ref):
    out_ref[...] = (own_ref[...].astype(f32) + received_ref[...].astype(f32)).astype(bf16)
    sent_ref[...] = later_ref[...]


def hidden_kernel(width, part, each, *refs):
    parts, out_ref = refs[:-1], refs[-1]
    total = functools.reduce(jnp.add, [ref[...].astype(f32) for ref in parts])
    side = total[-2:-1, :LANES] + total[-1:, :LANES]
    blocks = [(2 * i * each, i * each, each) for i in range(part // each)]
    for start, row, count in blocks + [(2 * part, part, out_ref.shape[0] - part)]:
        gates, ups = total[start : start + count], total[start + count : start + 2 * count]
        found = iota((count, LANES), 1) == iota((count, LANES), 0) + row
        squares = jnp.sum(jnp.where(found, side, 0.0), axis=1, keepdims=True)
        row_scale = lax.rsqrt(squares / width + epsilon)
        gates, ups = gates * row_scale, ups * row_scale
        out_ref[row : row + count, :] = (gates / (1.0 + jnp.exp(-gates)) * ups).astype(bf16)


def down_rows(distance, slots, hidden_ref, weight_ref):
    part = weight_ref.shape[0] * slots // lax.axis_size("head")
    each = min(slots, part)
    first = (lax.axis_index("head") ^ distance) * part
    return [
        dot(hidden_ref[i * each : (i + 1) * each, :], weight_ref[(first + i * each) // slots])
        for i in range(part // each)
    ]


def down_kernel(distance, slots, hidden_ref, weight_ref, out_ref):
    out_ref[...] = jnp.concatenate(down_rows(distance, slots, hidden_ref, weight_ref), axis=0)


def combine_kernel(distance, slots, coarse_ref, fine_ref, weight_ref, shared_weight_ref, *refs):
    head_devs = lax.axis_size("head")
    hidden_refs, done_refs = refs[:head_devs], refs[head_devs : 2 * head_devs - 1]
    routed_ref, shared_ref, rows_ref = refs[2 * head_devs - 1 :]
    me = lax.axis_index("head")
    part = weight_ref.shape[0] * slots // head_devs
    last = jnp.concatenate(
        down_rows(distance, slots, hidden_refs[distance], weight_ref), axis=0
    )
    done = {j: ref for j, ref in zip([j for j in range(head_devs) if j != distance], done_refs)}
    for j in range(head_devs):
        rows = pl.ds(pl.multiple_of((me ^ j) * part, TILE), part)
        rows_ref[rows, :] = last if j == distance else done[j][...]
    values = rows_ref[...]
    coarse = values.astype(bf16)
    fine = (values - coarse.astype(f32)).astype(bf16)
    def weighted(gates, rows):
        return lax.dot_general(gates, rows, over_rows, preferred_element_type=f32)

    gates = coarse_ref[...]
    routed = weighted(gates, coarse) + (weighted(gates, fine) + weighted(fine_ref[...], coarse))
    pools, req_dev, _ = routed_ref.shape
    for place in range(pools):
        routed_ref[place] = routed[place * req_dev : (place + 1) * req_dev].astype(bf16)
    share = shared_ref.shape[1]
    shared = jnp.concatenate([ref[part:, :].astype(f32) for ref in hidden_refs], axis=0)
    shared = dot(shared.astype(bf16), shared_weight_ref[0])
    for j in range(head_devs):
        shared_ref[me ^ j] = shared[j * share : (j + 1) * share]


def block_kernel(pieces_ref, shared_ref, after_ref, out_ref):
    req_dev = after_ref.shape[0]
    shared = jnp.concatenate([shared_ref[i] for i in range(shared_ref.shape[0])], axis=0)
    total = after_ref[...] + shared[:req_dev]
    for place in range(pieces_ref.shape[0]):
        total = total + pieces_ref[place].astype(f32)
    out_ref[...] = total.astype(bf16)


def join_kernel(bias_ref, *refs):
    for place, ref in enumerate(refs[:-1]):
        refs[-1][place] = ref[0]


def project_kernel(distances, width, begins, ends, gain_ref, weight_ref, *refs):
    me = lax.axis_index("head")
    count = len(distances)
    block_refs, refs = refs[:count], refs[count:]
    total, squares = 0.0, 0.0
    if not begins:
        total, squares = refs[0][...], refs[1][:, 0:1]
        refs = refs[2:]
    for distance, ref in zip(distances, block_refs):
        block = ref[...].astype(f32)
        col_part = block.shape[1]
        rows = pl.ds(pl.multiple_of((me ^ distance) * col_part, LANES), col_part)
        squares = squares + jnp.sum(block * block, axis=1, keepdims=True)
        scaled = (block * gain_columns(gain_ref, me ^ distance, col_part)).astype(bf16)
        total = total + dot(scaled, weight_ref[rows, :])
    if not ends:
        refs[0][...] = total
        refs[1][...] = jnp.broadcast_to(squares, refs[1].shape)
        return
    *every_refs, hidden_ref, out_ref = refs
    out_ref[...] = (total * lax.rsqrt(squares / width + epsilon)).astype(bf16)
    for distance, ref in enumerate(every_refs):
        columns = pl.ds(pl.multiple_of((me ^ distance) * ref.shape[1], LANES), ref.shape[1])
        hidden_ref[:, columns] = ref[...]


def per_device(
    queries,
    fresh_pair,
    cache_blocks,
    block_table,
    lengths,
    residual,
    w_output,
    norm_gain,
    routes,
    route_gates,
    w_gate_up,
    w_down,
    shared_gate_up,
    shared_down,
    next_gain,
    w_query_key_value,
):
    pools = lax.axis_size("pool")
    head_devs = lax.axis_size("head")
    req_dev, lane_width = queries.shape
    req_total = block_table.shape[0]
    blk_count, _, block_len, _ = cache_blocks.shape
    exp_dev, col_part, _, ffe = w_gate_up.shape
    width = residual.shape[1]
    slots = min(MOST * pools, req_total)
    slot_total = exp_dev * slots
    extra = -(-req_dev // TILE) * TILE
    part, share = slot_total // head_devs, -(-req_dev // head_devs)
    small = pools <= 8
    distances = list(range(1, head_devs))
    piece_experts = max(1, exp_dev // head_devs)
    fetch_shape = ((piece_experts, col_part, 2, ffe), bf16)
    fetched = list(reversed(range(2, head_devs)))

    queries = queries[None]
    table, counts = block_table.T, lengths[None, :]
    later = [queries, table, counts, cache_blocks, fresh_pair, residual, w_gate_up]
    (early,) = call(
        early_kernel,
        "early",
        [((1,), jnp.int32)],
        later,
        far=range(len(later)),
        megabytes=59,
    )
    (bias,) = call(
        functools.partial(setup_kernel, blk_count, block_len),
        "setup",
        [((req_total, blk_count * block_len), f32)],
        [early, table, counts],
        megabytes=4 + 16 * req_total * blk_count * block_len / 2**20,
    )
    if small:
        order = list(range(0, pools, 2))
        pieces = [queries] + [swap(queries, "pool", d) for d in order[1:]]
        (joined,) = call(
            join_kernel,
            "join_queries",
            [((len(order), req_dev, lane_width), bf16)],
            [bias] + pieces,
            far=[0],
        )
        pieces = [joined, swap(joined, "pool", 1)]
        order = order + [d + 1 for d in order]
    else:
        step = 1
        order, pieces = [0], [queries]
        while step < pools:
            whole = queries if step == 1 else jnp.concatenate(pieces, axis=0)
            pieces.append(swap(whole, "pool", step))
            order += [d ^ step for d in order]
            step *= 2
    (partial,) = call(
        functools.partial(attention_kernel, order),
        "attention",
        [((req_total, lane_width + LANES), bf16)],
        [cache_blocks, bias, fresh_pair, residual] + pieces,
        scratch=[((pools, req_dev, lane_width), f32)],
        megabytes=4 + 32 * req_total * blk_count * block_len / 2**20,
    )
    parts = lax.all_gather(partial, "pool", axis=0)
    sums = call(
        functools.partial(merge_kernel, req_dev),
        "merge_project",
        [((req_total, col_part), f32)] + [((req_total, col_part), bf16)] * (head_devs - 1),
        [parts, w_output],
        scratch=[((req_total, lane_width), bf16)],
        megabytes=5 + 12 * pools * req_total * LANES / 2**20,
    )
    pick, gate_coarse, gate_fine, spread, *weights = call(
        functools.partial(routing_kernel, fetched, slots, req_dev),
        "routing",
        [
            ((slot_total + extra, req_total), bf16),
            ((slot_total, req_total), bf16),
            ((slot_total, req_total), bf16),
            ((col_part, 2 * col_part), bf16),
        ]
        + [fetch_shape] * len(fetched),
        [routes.T, route_gates.T, sums[0], w_gate_up],
        far=[3],
        copies=[len(fetched) * piece_experts * SPLIT],
        megabytes=24,
        moved=2e7,
    )
    weights = dict(zip(fetched, weights))
    received = {d: swap(sums[d], "head", d) for d in reversed(distances)}
    gate_rows, up_rows, side, own_after = call(
        functools.partial(prepare_kernel, req_dev, part, share),
        "prepare",
        [
            ((slot_total + extra, 2 * col_part), bf16),
            ((slot_total + extra, 2 * col_part), bf16),
            ((head_devs, 8, LANES), f32),
            ((req_dev, col_part), f32),
        ],
        [norm_gain.reshape(-1, LANES), pick, spread, sums[0]] + [received[d] for d in distances],
        scratch=[((pools, req_dev, col_part), f32)],
        megabytes=6,
    )

    piece = part + share
    piece_shape = ((2 * piece + 2, ffe), bf16)
    shared_shape = ((head_devs, 2 * share, ffe), f32)
    shared_rows = None
    last = head_devs - 1

    def experts(distance, after=()):
        nonlocal shared_rows
        args = [gate_rows, up_rows, side, weights.get(distance, w_gate_up)]
        outs, scratch, copies, far = [piece_shape], [], [], []
        if shared_rows is None:
            args, outs = args + [shared_gate_up], outs + [shared_shape]
        else:
            args = args + [shared_rows] + list(after)
        if distance < 2:
            scratch, copies, far = [fetch_shape], [piece_experts * SPLIT], [3]
        mine, *shared = call(
            functools.partial(expert_kernel, distance, slots, part, len(outs) > 1),
            f"experts_{distance}",
            outs,
            args,
            scratch=scratch,
            copies=copies,
            far=far,
            megabytes=32 if distance < 2 else 10,
        )
        if shared:
            (shared_rows,) = shared
        return mine

    if head_devs == 4:
        near = swap(experts(2), "head", 1)
        own_near = experts(1)
        pair, own_near = call(
            add_kernel,
            "add_pair",
            [piece_shape, piece_shape],
            [experts(3, [own_near]), near, own_near],
        )
        far = swap(pair, "head", 3)
        parts = [experts(0, [pair]), far, swap(own_near, "head", 1)]
    else:
        parts = [swap(experts(d), "head", d) for d in reversed(range(1, head_devs))]
        parts = [experts(0)] + parts
    (hidden,) = call(
        functools.partial(hidden_kernel, width, part, min(slots, part)),
        "hidden",
        [((piece, ffe), bf16)],
        parts,
    )
    hiddens = {0: hidden}
    for d in distances:
        hiddens[d] = swap(hidden, "head", d)
    done = []
    for d in range(last):
        done += call(
            functools.partial(down_kernel, d, slots),
            f"down_{d}",
            [((slot_total // head_devs, col_part), f32)],
            [hiddens[d], w_down],
            megabytes=6,
            )
    routed, shared_out = call(
        functools.partial(combine_kernel, last, slots),
        "combine",
        [((pools, req_dev, col_part), bf16), ((head_devs, share, col_part), f32)],
        [gate_coarse, gate_fine, w_down, shared_down]
        + [hiddens[d] for d in range(head_devs)]
        + done,
        scratch=[((slot_total, col_part), f32)],
        megabytes=6,
    )
    pieces = lax.all_to_all(routed, "pool", 0, 0)
    (block,) = call(
        block_kernel,
        "block",
        [((req_dev, col_part), bf16)],
        [pieces, shared_out, own_after],
        megabytes=4,
    )
    blocks = [block] + [swap(block, "head", d) for d in distances]
    last_args = [next_gain.reshape(-1, LANES), w_query_key_value]
    out_width = w_query_key_value.shape[1]
    running = []
    for which in ([0], distances[2:]):
        running = call(
            functools.partial(project_kernel, which, width, not running, False),
            f"project_{which[0]}",
            [((req_dev, out_width), f32), ((req_dev, LANES), f32)],
            last_args + [blocks[d] for d in which] + list(running),
            megabytes=6,
        )
    next_hidden, next_projection = call(
        functools.partial(project_kernel, distances[:2], width, False, True),
        "project",
        [((req_dev, width), bf16), ((req_dev, out_width), bf16)],
        last_args + [blocks[d] for d in distances[:2]] + list(running) + blocks,
        megabytes=6,
    )
    return (next_hidden, next_projection)


def solution(mesh):
    in_specs = (
        P("pool", "head"),
        P("pool", None, "head"),
        P("pool", None, None, "head"),
        P(),
        P(),
        P("pool", None),
        P("head", None),
        P(),
        P(),
        P(),
        P("pool", "head", None, None),
        P("pool", None, "head"),
        P(None, "head", None, None),
        P(None, None, "head"),
        P(),
        P(None, "head"),
    )
    out_specs = (P("pool", None), P("pool", "head"))
    return jax.shard_map(
        per_device, mesh=mesh, in_specs=in_specs, out_specs=out_specs, check_vma=False
    )
```

```python
import functools
import math

import jax
import jax.numpy as jnp
from jax import lax
from jax.experimental import pallas as pl
from jax.experimental.pallas import tpu as pltpu
from jax.sharding import PartitionSpec as P

HD = 128
LANES = 128
TILE = 16
MOST = 2
SPLIT = 4
HALF = LANES // 2


epsilon = 1e-06
floor_score = -1e30
least_score = -1e29
bf16 = jnp.bfloat16
f32 = jnp.float32
over_rows = (((0,), (0,)), ((), ()))
VMEM = pl.BlockSpec(memory_space=pltpu.VMEM)
SMEM = pl.BlockSpec(memory_space=pltpu.SMEM)
FAR = pl.BlockSpec(memory_space=pltpu.HBM)


def iota(shape, dim):
    return lax.broadcasted_iota(jnp.int32, shape, dim)


def one_hot(mask):
    return mask.astype(f32).astype(bf16)


def dot(left, right):
    return jnp.dot(left, right, preferred_element_type=f32)


def place(shape):
    return SMEM if shape == (1,) else VMEM


def call(kernel, name, outs, args, scratch=(), copies=(), far=(), megabytes=4, moved=1e5):
    semaphores = [pltpu.SemaphoreType.DMA((count,)) for count in copies]
    return pl.pallas_call(
        kernel,
        out_shape=[jax.ShapeDtypeStruct(shape, dtype) for shape, dtype in outs],
        in_specs=[FAR if i in far else place(arg.shape) for i, arg in enumerate(args)],
        out_specs=[place(shape) for shape, _ in outs],
        scratch_shapes=[pltpu.VMEM(shape, dtype) for shape, dtype in scratch] + semaphores,
        compiler_params=pltpu.CompilerParams(vmem_limit_bytes=int(megabytes * 2**20)),
        cost_estimate=pl.CostEstimate(
            flops=1000, bytes_accessed=int(moved), transcendentals=0
        ),
        name=name,
    )(*args)


def swap(value, axis, distance):
    count = lax.axis_size(axis)
    return lax.ppermute(value, axis, [(i, i ^ distance) for i in range(count)])


def start_weights(distance, slots, weight_ref, out_ref, semaphores, skip=0):
    count, depth = out_ref.shape[:2]
    part = weight_ref.shape[0] * slots // lax.axis_size("head")
    first = (lax.axis_index("head") ^ distance) * part // slots
    rows = depth // SPLIT
    copies = [
        pltpu.make_async_copy(
            weight_ref.at[first + skip + i, pl.ds(k * rows, rows)],
            out_ref.at[i, pl.ds(k * rows, rows)],
            semaphores.at[i * SPLIT + k],
        )
        for i in range(count)
        for k in range(SPLIT)
    ]
    for copy in copies:
        copy.start()
    return copies


def start_all_weights(distances, slots, weight_ref, out_refs, semaphores):
    copies, used = [], 0
    for distance, out_ref in zip(distances, out_refs):
        count = out_ref.shape[0] * SPLIT
        own = semaphores.at[pl.ds(used, count)]
        used += count
        copies += start_weights(distance, slots, weight_ref, out_ref, own)
    return copies


def early_kernel(*refs):
    refs[-1][0] = 0


def setup_kernel(blocks, block_len, early_ref, table_ref, length_ref, bias_ref):
    pool_idx = lax.axis_index("pool")
    list_len, req_total = table_ref.shape
    tokens = blocks * block_len
    table = table_ref[...] - pool_idx * blocks
    left = length_ref[...] - iota((list_len, req_total), 0) * block_len
    block_row = iota((LANES, req_total), 0)
    limits = jnp.zeros((LANES, req_total), f32)
    for block in range(blocks):
        found = jnp.sum(jnp.where(table == block, left, 0).astype(f32), axis=0, keepdims=True)
        limits = jnp.where(block_row == block, found, limits)
    limits = jnp.clip(limits, 0.0, float(block_len)).astype(bf16)
    expand = iota((LANES, tokens), 1) // block_len == iota((LANES, tokens), 0)
    limits = lax.dot_general(limits, one_hot(expand), over_rows, preferred_element_type=f32)
    within = lax.rem(iota((1, tokens), 1), block_len).astype(f32)
    bias_ref[...] = jnp.where(within < limits, 0.0, floor_score)


def attention_kernel(
    order,
    cache_ref,
    bias_ref,
    fresh_ref,
    residual_ref,
    *refs,
):
    *query_refs, out_ref, queries_ref = refs
    blocks, _, block_len, _ = cache_ref.shape
    pool_idx = lax.axis_index("pool")
    pools, req_dev, lane_width = queries_ref.shape
    req_total = pools * req_dev
    tokens = blocks * block_len
    scale = math.log2(math.e) / math.sqrt(HD)
    bias = bias_ref[...]
    pieces = [ref[i] for ref in query_refs for i in range(ref.shape[0])]
    for distance, piece in zip(order, pieces):
        queries_ref[pool_idx ^ distance] = piece.astype(f32)
    queries = jnp.concatenate([queries_ref[i] for i in range(pools)], axis=0).astype(bf16)
    own = iota((req_total, req_dev), 0) == iota((req_total, req_dev), 1) + pool_idx * req_dev
    own_bias = jnp.where(own, 0.0, floor_score)
    lane = iota((req_total, LANES), 1)
    side = jnp.zeros((req_total, LANES), f32)
    heads = lane_width // HD
    contract = (((1,), (1,)), ((), ()))
    for head in range(heads):
        columns = slice(head * HD, (head + 1) * HD)
        query = queries[:, columns]
        keys = cache_ref[:, 0, :, columns].reshape(tokens, HD)
        scores = lax.dot_general(query, keys, contract, preferred_element_type=f32) * scale + bias
        new_scores = (
            lax.dot_general(query, fresh_ref[:, 0, columns], contract, preferred_element_type=f32)
            * scale
            + own_bias
        )
        top = jnp.maximum(
            jnp.max(scores, axis=1, keepdims=True), jnp.max(new_scores, axis=1, keepdims=True)
        )
        top = jnp.maximum(top, least_score).astype(bf16).astype(f32)
        weights = jnp.exp2(scores - top)
        new_weights = jnp.exp2(new_scores - top)
        total = jnp.sum(weights, axis=1, keepdims=True) + jnp.sum(
            new_weights, axis=1, keepdims=True
        )
        values = cache_ref[:, 1, :, columns].reshape(tokens, HD)
        mixed = dot(weights.astype(bf16), values) + dot(
            new_weights.astype(bf16), fresh_ref[:, 1, columns]
        )
        inverse = jnp.where(total > 0.0, 1.0 / jnp.where(total > 0.0, total, 1.0), 0.0)
        out_ref[:, columns] = (mixed * inverse).astype(bf16)
        coarse = total.astype(bf16).astype(f32)
        side = jnp.where(lane == head, top, side)
        side = jnp.where(lane == heads + head, coarse, side)
        side = jnp.where(lane == 2 * heads + head, total - coarse, side)
    out_ref[:, lane_width:] = side.astype(bf16)
    start = pl.multiple_of(lax.axis_index("head") * lane_width, LANES)
    residual = residual_ref[:, pl.ds(start, lane_width)]
    for i in range(lane_width // HALF):
        rows = slice(i * req_dev, (i + 1) * req_dev)
        out_ref[rows, lane_width + HALF :] = residual[:, i * HALF : (i + 1) * HALF]


def merge_kernel(req_dev, parts_ref, weight_ref, *refs):
    out_refs, attended_ref = refs[:-1], refs[-1]
    count, req_total, packed = parts_ref.shape
    col_part = out_refs[0].shape[1]
    lane_width = packed - LANES
    heads = lane_width // HD
    me = lax.axis_index("head")
    sides = [parts_ref[i, :, lane_width:].astype(f32) for i in range(count)]
    lane = iota((req_total, LANES), 1)
    tops = [jnp.where(lane < heads, side, 0.0) for side in sides]
    top = functools.reduce(jnp.maximum, tops)

    def shifted(side, by):
        return pltpu.roll(side, LANES - by, 1)

    shares = [
        (shifted(side, heads) + shifted(side, 2 * heads)) * jnp.exp2(part - top)
        for side, part in zip(sides, tops)
    ]
    denominator = functools.reduce(jnp.add, shares)
    inverse = 1.0 / jnp.where(lane < heads, denominator, 1.0)
    spread = iota((2 * LANES, lane_width), 1) // HD == lax.rem(
        iota((2 * LANES, lane_width), 0), LANES
    )
    spread = one_hot(spread)
    mixed = jnp.zeros((req_total, lane_width), f32)
    for i, share in enumerate(shares):
        share = jnp.where(lane < heads, share * inverse, 0.0)
        coarse = share.astype(bf16)
        fine = (share - coarse.astype(f32)).astype(bf16)
        weight = dot(jnp.concatenate([coarse, fine], axis=1), spread)
        mixed = mixed + weight * parts_ref[i, :, :lane_width].astype(f32)
    attended_ref[...] = mixed.astype(bf16)
    for distance, out_ref in enumerate(out_refs):
        start = pl.multiple_of((me ^ distance) * col_part, LANES)
        projected = dot(attended_ref[...], weight_ref[:, pl.ds(start, col_part)])
        out_ref[...] = projected.astype(out_ref.dtype)
    for i, side in enumerate(sides):
        rows = slice(i * req_dev, (i + 1) * req_dev)
        pieces = [
            side[k * req_dev : (k + 1) * req_dev, HALF:] for k in range(lane_width // HALF)
        ]
        out_refs[0][rows, :] = out_refs[0][rows, :] + jnp.concatenate(pieces, axis=1)


def routing_kernel(
    distances,
    slots,
    req_dev,
    routes_ref,
    gates_ref,
    after_ref,
    far_weight_ref,
    pick_ref,
    coarse_ref,
    fine_ref,
    spread_ref,
    *refs,
):
    weight_refs, semaphores = refs[:-1], refs[-1]
    fetched = start_all_weights(distances, slots, far_weight_ref, weight_refs, semaphores)
    top_k, req_total = routes_ref.shape
    slot_total = coarse_ref.shape[0]
    extra = pick_ref.shape[0] - slot_total
    pool_idx = lax.axis_index("pool")
    expert = iota((slot_total, req_total), 0) // slots + pool_idx * (slot_total // slots)
    rank = lax.rem(iota((slot_total, req_total), 0), slots).astype(f32)
    chosen = jnp.zeros((slot_total, req_total), f32)
    gate = jnp.zeros((slot_total, req_total), f32)
    for k in range(top_k):
        match = routes_ref[k : k + 1, :] == expert
        chosen = jnp.where(match, 1.0, chosen)
        gate = jnp.where(match, gates_ref[k : k + 1, :], gate)
    earlier = iota((req_total, req_total), 0) < iota((req_total, req_total), 1)
    place = dot(chosen.astype(bf16), one_hot(earlier))
    pick = jnp.where(place == rank, chosen, 0.0)
    pick_ref[:slot_total, :] = pick.astype(bf16)
    own_place = iota((extra, req_total), 0)
    own = iota((extra, req_total), 1) == own_place + pool_idx * req_dev
    pick_ref[slot_total:, :] = one_hot(jnp.logical_and(own, own_place < req_dev))
    gate = gate * pick
    coarse = gate.astype(bf16)
    coarse_ref[...] = coarse
    fine_ref[...] = (gate - coarse.astype(f32)).astype(bf16)
    spread_ref[...] = one_hot(iota(spread_ref.shape, 1) == 2 * iota(spread_ref.shape, 0))
    for copy in fetched:
        copy.wait()


def gain_columns(gain_ref, part, count):
    gains = gain_ref[...].astype(f32)
    rows = iota(gains.shape, 0)
    first = part * (count // LANES)
    return jnp.concatenate(
        [
            jnp.sum(jnp.where(rows == first + i, gains, 0.0), axis=0, keepdims=True)
            for i in range(count // LANES)
        ],
        axis=1,
    )


def prepare_kernel(req_dev, part, share, gain_ref, pick_ref, spread_ref, own_sum_ref, *refs):
    received, (gate_ref, up_ref, side_ref, after_ref, all_ref) = refs[:-5], refs[-5:]
    req_total, col_part = own_sum_ref.shape
    after = own_sum_ref[...]
    for ref in received:
        after = after + ref[...].astype(f32)
    for place in range(all_ref.shape[0]):
        all_ref[place] = after[place * req_dev : (place + 1) * req_dev]
    after_ref[...] = all_ref[lax.axis_index("pool")]
    gains = gain_columns(gain_ref, lax.axis_index("head"), col_part)
    scaled = (after * gains).astype(bf16)
    squares = jnp.sum(after * after, axis=1, keepdims=True)
    coarse = squares.astype(bf16).astype(f32)
    lane = iota((req_total, LANES), 1)
    side = jnp.where(lane == 0, coarse, jnp.where(lane == 1, squares - coarse, 0.0))
    pick = pick_ref[...]
    picked = dot(pick, scaled).astype(bf16)
    same = iota((req_total, req_total), 0) == iota((req_total, req_total), 1)
    turned = lax.dot_general(
        side.astype(bf16), one_hot(same), over_rows, preferred_element_type=f32
    )[:8].astype(bf16)
    contract = (((1,), (1,)), ((), ()))
    lined = lax.dot_general(turned, pick, contract, preferred_element_type=f32)
    targets = side_ref.shape[0]
    for target in range(targets):
        first = targets * part + target * share
        side_ref[target] = jnp.zeros(side_ref.shape[1:], f32)
        side_ref[target, :, :part] = lined[:, target * part : (target + 1) * part]
        side_ref[target, :, part : part + share] = lined[:, first : first + share]
    spread = dot(picked, spread_ref[...])
    gate_ref[...] = spread.astype(bf16)
    up_ref[...] = pltpu.roll(spread, 1, 1).astype(bf16)


def expert_kernel(
    distance, slots, part, makes_shared, gate_ref, up_ref, side_ref, weight_ref, *refs
):
    refs = list(refs)
    head_devs = lax.axis_size("head")
    weight_refs = [weight_ref]
    if distance < 2:
        near_ref, semaphores = refs[-2:]
        refs = refs[:-2]
        ahead = part // min(slots, part) - near_ref.shape[0]
        fetched = start_weights(distance, slots, weight_ref, near_ref, semaphores, ahead)
        weight_refs = [near_ref]
        if ahead:
            weight_refs = [refs.pop(0), near_ref]
        for copy in fetched:
            copy.wait()
    near_weights = [ref.at[i] for ref in weight_refs for i in range(ref.shape[0])]
    _, depth, _, ffe = weight_ref.shape
    target = lax.axis_index("head") ^ distance
    if makes_shared:
        shared_weight_ref, out_ref, shared_ref = refs
        share = shared_ref.shape[1] // 2
        extra = gate_ref.shape[0] - part * head_devs
        first = part * head_devs
        lhs = jnp.concatenate([gate_ref[first:, :], up_ref[first:, :]], axis=0)
        sums = dot(lhs, shared_weight_ref[0].reshape(2 * depth, ffe))
        for place in range(head_devs):
            rows = slice(place * share, (place + 1) * share)
            shared_ref[place, :share, :] = sums[:extra][rows]
            shared_ref[place, share:, :] = sums[extra:][rows]
    else:
        shared_ref, out_ref = refs[0], refs[-1]
    each = min(slots, part)
    for i in range(part // each):
        rows = pl.ds(pl.multiple_of(target * part + i * each, TILE), each)
        lhs = jnp.concatenate([gate_ref[rows, :], up_ref[rows, :]], axis=0)
        sums = dot(lhs, near_weights[i][...].reshape(2 * depth, ffe))
        out_ref[2 * i * each : 2 * (i + 1) * each, :] = sums.astype(bf16)
    side = side_ref[target][:2]
    side = jnp.concatenate([side, jnp.zeros((2, ffe - LANES), f32)], axis=1)
    last = jnp.concatenate([shared_ref[target], side], axis=0)
    out_ref[2 * part :, :] = last.astype(bf16)


def add_kernel(own_ref, received_ref, later_ref, out_ref, sent_ref):
    out_ref[...] = (own_ref[...].astype(f32) + received_ref[...].astype(f32)).astype(bf16)
    sent_ref[...] = later_ref[...]


def hidden_kernel(width, part, each, *refs):
    parts, out_ref = refs[:-1], refs[-1]
    total = functools.reduce(jnp.add, [ref[...].astype(f32) for ref in parts])
    side = total[-2:-1, :LANES] + total[-1:, :LANES]
    blocks = [(2 * i * each, i * each, each) for i in range(part // each)]
    for start, row, count in blocks + [(2 * part, part, out_ref.shape[0] - part)]:
        gates, ups = total[start : start + count], total[start + count : start + 2 * count]
        found = iota((count, LANES), 1) == iota((count, LANES), 0) + row
        squares = jnp.sum(jnp.where(found, side, 0.0), axis=1, keepdims=True)
        row_scale = lax.rsqrt(squares / width + epsilon)
        gates, ups = gates * row_scale, ups * row_scale
        out_ref[row : row + count, :] = (gates / (1.0 + jnp.exp(-gates)) * ups).astype(bf16)


def down_rows(distance, slots, hidden_ref, weight_ref):
    part = weight_ref.shape[0] * slots // lax.axis_size("head")
    each = min(slots, part)
    first = (lax.axis_index("head") ^ distance) * part
    return [
        dot(hidden_ref[i * each : (i + 1) * each, :], weight_ref[(first + i * each) // slots])
        for i in range(part // each)
    ]


def down_kernel(distance, slots, hidden_ref, weight_ref, out_ref):
    out_ref[...] = jnp.concatenate(down_rows(distance, slots, hidden_ref, weight_ref), axis=0)


def combine_kernel(distance, slots, coarse_ref, fine_ref, weight_ref, shared_weight_ref, *refs):
    head_devs = lax.axis_size("head")
    hidden_refs, done_refs = refs[:head_devs], refs[head_devs : 2 * head_devs - 1]
    routed_ref, shared_ref, rows_ref = refs[2 * head_devs - 1 :]
    me = lax.axis_index("head")
    part = weight_ref.shape[0] * slots // head_devs
    last = jnp.concatenate(
        down_rows(distance, slots, hidden_refs[distance], weight_ref), axis=0
    )
    done = {j: ref for j, ref in zip([j for j in range(head_devs) if j != distance], done_refs)}
    for j in range(head_devs):
        rows = pl.ds(pl.multiple_of((me ^ j) * part, TILE), part)
        rows_ref[rows, :] = last if j == distance else done[j][...]
    values = rows_ref[...]
    coarse = values.astype(bf16)
    fine = (values - coarse.astype(f32)).astype(bf16)
    def weighted(gates, rows):
        return lax.dot_general(gates, rows, over_rows, preferred_element_type=f32)

    gates = coarse_ref[...]
    routed = weighted(gates, coarse) + (weighted(gates, fine) + weighted(fine_ref[...], coarse))
    pools, req_dev, _ = routed_ref.shape
    for place in range(pools):
        routed_ref[place] = routed[place * req_dev : (place + 1) * req_dev].astype(bf16)
    share = shared_ref.shape[1]
    shared = jnp.concatenate([ref[part:, :].astype(f32) for ref in hidden_refs], axis=0)
    shared = dot(shared.astype(bf16), shared_weight_ref[0])
    for j in range(head_devs):
        shared_ref[me ^ j] = shared[j * share : (j + 1) * share]


def block_kernel(pieces_ref, shared_ref, after_ref, out_ref):
    req_dev = after_ref.shape[0]
    shared = jnp.concatenate([shared_ref[i] for i in range(shared_ref.shape[0])], axis=0)
    total = after_ref[...] + shared[:req_dev]
    for place in range(pieces_ref.shape[0]):
        total = total + pieces_ref[place].astype(f32)
    out_ref[...] = total.astype(bf16)


def join_kernel(bias_ref, *refs):
    for place, ref in enumerate(refs[:-1]):
        refs[-1][place] = ref[0]


def project_kernel(distances, width, begins, ends, gain_ref, weight_ref, *refs):
    me = lax.axis_index("head")
    count = len(distances)
    block_refs, refs = refs[:count], refs[count:]
    total, squares = 0.0, 0.0
    if not begins:
        total, squares = refs[0][...], refs[1][:, 0:1]
        refs = refs[2:]
    for distance, ref in zip(distances, block_refs):
        block = ref[...].astype(f32)
        col_part = block.shape[1]
        rows = pl.ds(pl.multiple_of((me ^ distance) * col_part, LANES), col_part)
        squares = squares + jnp.sum(block * block, axis=1, keepdims=True)
        scaled = (block * gain_columns(gain_ref, me ^ distance, col_part)).astype(bf16)
        total = total + dot(scaled, weight_ref[rows, :])
    if not ends:
        refs[0][...] = total
        refs[1][...] = jnp.broadcast_to(squares, refs[1].shape)
        return
    *every_refs, hidden_ref, out_ref = refs
    out_ref[...] = (total * lax.rsqrt(squares / width + epsilon)).astype(bf16)
    for distance, ref in enumerate(every_refs):
        columns = pl.ds(pl.multiple_of((me ^ distance) * ref.shape[1], LANES), ref.shape[1])
        hidden_ref[:, columns] = ref[...]


def per_device(
    queries,
    fresh_pair,
    cache_blocks,
    block_table,
    lengths,
    residual,
    w_output,
    norm_gain,
    routes,
    route_gates,
    w_gate_up,
    w_down,
    shared_gate_up,
    shared_down,
    next_gain,
    w_query_key_value,
):
    pools = lax.axis_size("pool")
    head_devs = lax.axis_size("head")
    req_dev, lane_width = queries.shape
    req_total = block_table.shape[0]
    blk_count, _, block_len, _ = cache_blocks.shape
    exp_dev, col_part, _, ffe = w_gate_up.shape
    width = residual.shape[1]
    slots = min(MOST * pools, req_total)
    slot_total = exp_dev * slots
    extra = -(-req_dev // TILE) * TILE
    part, share = slot_total // head_devs, -(-req_dev // head_devs)
    small = pools <= 8
    distances = list(range(1, head_devs))
    piece_experts = max(1, exp_dev // head_devs)
    fetch_shape = ((piece_experts, col_part, 2, ffe), bf16)
    fetched = list(reversed(range(2, head_devs)))
    ahead = piece_experts // 2

    queries = queries[None]
    table, counts = block_table.T, lengths[None, :]
    later = [queries, table, counts, cache_blocks, fresh_pair, residual, w_gate_up]
    (early,) = call(
        early_kernel,
        "early",
        [((1,), jnp.int32)],
        later,
        far=range(len(later)),
        megabytes=59,
    )
    (bias,) = call(
        functools.partial(setup_kernel, blk_count, block_len),
        "setup",
        [((req_total, blk_count * block_len), f32)],
        [early, table, counts],
        megabytes=4 + 16 * req_total * blk_count * block_len / 2**20,
    )
    if small:
        order = list(range(0, pools, 2))
        pieces = [queries] + [swap(queries, "pool", d) for d in order[1:]]
        (joined,) = call(
            join_kernel,
            "join_queries",
            [((len(order), req_dev, lane_width), bf16)],
            [bias] + pieces,
            far=[0],
        )
        pieces = [joined, swap(joined, "pool", 1)]
        order = order + [d + 1 for d in order]
    else:
        step = 1
        order, pieces = [0], [queries]
        while step < pools:
            whole = queries if step == 1 else jnp.concatenate(pieces, axis=0)
            pieces.append(swap(whole, "pool", step))
            order += [d ^ step for d in order]
            step *= 2
    (partial,) = call(
        functools.partial(attention_kernel, order),
        "attention",
        [((req_total, lane_width + LANES), bf16)],
        [cache_blocks, bias, fresh_pair, residual] + pieces,
        scratch=[((pools, req_dev, lane_width), f32)],
        megabytes=4 + 32 * req_total * blk_count * block_len / 2**20,
    )
    parts = lax.all_gather(partial, "pool", axis=0)
    sums = call(
        functools.partial(merge_kernel, req_dev),
        "merge_project",
        [((req_total, col_part), f32)] + [((req_total, col_part), bf16)] * (head_devs - 1),
        [parts, w_output],
        scratch=[((req_total, lane_width), bf16)],
        megabytes=5 + 12 * pools * req_total * LANES / 2**20,
    )
    pick, gate_coarse, gate_fine, spread, *weights = call(
        functools.partial(routing_kernel, fetched + [1] * bool(ahead), slots, req_dev),
        "routing",
        [
            ((slot_total + extra, req_total), bf16),
            ((slot_total, req_total), bf16),
            ((slot_total, req_total), bf16),
            ((col_part, 2 * col_part), bf16),
        ]
        + [fetch_shape] * len(fetched)
        + [((ahead,) + fetch_shape[0][1:], bf16)] * bool(ahead),
        [routes.T, route_gates.T, sums[0], w_gate_up],
        far=[3],
        copies=[(len(fetched) * piece_experts + ahead) * SPLIT],
        megabytes=24,
        moved=2e7,
    )
    first_near = weights[len(fetched) :]
    weights = dict(zip(fetched, weights))
    received = {d: swap(sums[d], "head", d) for d in reversed(distances)}
    gate_rows, up_rows, side, own_after = call(
        functools.partial(prepare_kernel, req_dev, part, share),
        "prepare",
        [
            ((slot_total + extra, 2 * col_part), bf16),
            ((slot_total + extra, 2 * col_part), bf16),
            ((head_devs, 8, LANES), f32),
            ((req_dev, col_part), f32),
        ],
        [norm_gain.reshape(-1, LANES), pick, spread, sums[0]] + [received[d] for d in distances],
        scratch=[((pools, req_dev, col_part), f32)],
        megabytes=6,
    )

    piece = part + share
    piece_shape = ((2 * piece + 2, ffe), bf16)
    shared_shape = ((head_devs, 2 * share, ffe), f32)
    shared_rows = None
    last = head_devs - 1

    def experts(distance, after=()):
        nonlocal shared_rows
        args = [gate_rows, up_rows, side, weights.get(distance, w_gate_up)]
        outs, scratch, copies, far = [piece_shape], [], [], []
        if shared_rows is None:
            args, outs = args + [shared_gate_up], outs + [shared_shape]
        else:
            args = args + [shared_rows] + list(after)
        if distance < 2:
            given = list(first_near) if distance == 1 else []
            args = args[:4] + given + args[4:]
            rest = piece_experts - len(given) * ahead
            scratch = [((rest,) + fetch_shape[0][1:], bf16)]
            copies, far = [rest * SPLIT], [3]
        mine, *shared = call(
            functools.partial(expert_kernel, distance, slots, part, len(outs) > 1),
            f"experts_{distance}",
            outs,
            args,
            scratch=scratch,
            copies=copies,
            far=far,
            megabytes=32 if distance < 2 else 10,
        )
        if shared:
            (shared_rows,) = shared
        return mine

    if head_devs == 4:
        near = swap(experts(2), "head", 1)
        own_near = experts(1)
        pair, own_near = call(
            add_kernel,
            "add_pair",
            [piece_shape, piece_shape],
            [experts(3, [own_near]), near, own_near],
        )
        far = swap(pair, "head", 3)
        parts = [experts(0, [pair]), far, swap(own_near, "head", 1)]
    else:
        parts = [swap(experts(d), "head", d) for d in reversed(range(1, head_devs))]
        parts = [experts(0)] + parts
    (hidden,) = call(
        functools.partial(hidden_kernel, width, part, min(slots, part)),
        "hidden",
        [((piece, ffe), bf16)],
        parts,
    )
    hiddens = {0: hidden}
    for d in distances:
        hiddens[d] = swap(hidden, "head", d)
    done = []
    for d in range(last):
        done += call(
            functools.partial(down_kernel, d, slots),
            f"down_{d}",
            [((slot_total // head_devs, col_part), f32)],
            [hiddens[d], w_down],
            megabytes=6,
            )
    routed, shared_out = call(
        functools.partial(combine_kernel, last, slots),
        "combine",
        [((pools, req_dev, col_part), bf16), ((head_devs, share, col_part), f32)],
        [gate_coarse, gate_fine, w_down, shared_down]
        + [hiddens[d] for d in range(head_devs)]
        + done,
        scratch=[((slot_total, col_part), f32)],
        megabytes=6,
    )
    pieces = lax.all_to_all(routed, "pool", 0, 0)
    (block,) = call(
        block_kernel,
        "block",
        [((req_dev, col_part), bf16)],
        [pieces, shared_out, own_after],
        megabytes=4,
    )
    blocks = [block] + [swap(block, "head", d) for d in distances]
    last_args = [next_gain.reshape(-1, LANES), w_query_key_value]
    out_width = w_query_key_value.shape[1]
    running = []
    for which in ([0], distances[2:]):
        running = call(
            functools.partial(project_kernel, which, width, not running, False),
            f"project_{which[0]}",
            [((req_dev, out_width), f32), ((req_dev, LANES), f32)],
            last_args + [blocks[d] for d in which] + list(running),
            megabytes=6,
        )
    next_hidden, next_projection = call(
        functools.partial(project_kernel, distances[:2], width, False, True),
        "project",
        [((req_dev, width), bf16), ((req_dev, out_width), bf16)],
        last_args + [blocks[d] for d in distances[:2]] + list(running) + blocks,
        megabytes=6,
    )
    return (next_hidden, next_projection)


def solution(mesh):
    in_specs = (
        P("pool", "head"),
        P("pool", None, "head"),
        P("pool", None, None, "head"),
        P(),
        P(),
        P("pool", None),
        P("head", None),
        P(),
        P(),
        P(),
        P("pool", "head", None, None),
        P("pool", None, "head"),
        P(None, "head", None, None),
        P(None, None, "head"),
        P(),
        P(None, "head"),
    )
    out_specs = (P("pool", None), P("pool", "head"))
    return jax.shard_map(
        per_device, mesh=mesh, in_specs=in_specs, out_specs=out_specs, check_vma=False
    )
```
